32 devices in a mesh: row: 4 (over y, x), seq: 8 (over z, core).
Axes of the slice: x: 2, y: 2, z: 4, core: 2. Of those that a mesh axis runs over, the one named last changes fastest.
Arguments:
- mixer_input: bfloat16 [8192, 4352], P(('row', 'seq')), parts along dimension 0, may hold values from -6 to 6
- gate_input: bfloat16 [8192, 4096], P(('row', 'seq')), parts along dimension 0, may hold values from -6 to 6
- conv_forward: float32 [4, 4352], replicated, may hold values from -3 to 3
- conv_reverse: float32 [4, 4352], replicated, may hold values from -3 to 3
- step_size: float32 [64, 8192], P(None, ('row', 'seq')), parts along dimension 1, may hold values from 0 to 1, as said below
- decay_rate: float32 [256], P('row'), parts along dimension 0, may hold values from 1 to 8, as said below
- skip_scale: float32 [64], replicated, may hold values from 0.5 to 1.5
- norm_gain: float32 [4096], replicated, may hold values from 0.5 to 1.5
Outputs:
- mixer_output: bfloat16 [8192, 4096], P(('row', 'seq')), parts along dimension 0
The draws below stay inside these ranges and needn't reach their ends.
There are 4 independent parts, one for each index of `row`. The reference program is written for one: setup_inputs(seed, part) draws one part's arguments, and reference() takes and returns one part's arrays. A program takes and returns all parts, laid end to end along the dimension named above; an argument that names none is the same for every part. Nothing has to cross between parts.
Inputs may be any that keep to these rules, and one draw needn't show every extreme that they name: `step_size`: positive step sizes. `decay_rate`: positive coefficients.
All inputs are finite; a program needn't handle non-finite values.
Results may differ from the reference program's by a relative error of at most 0.007.
Values may be sent and summed in bfloat16 or wider, within the bound.
A program may use at most 192 MiB of HBM per device.

```python
import math
import jax
import jax.numpy as jnp
from jax import lax

HEADS = 64
HEAD_DIM = 64
STATE = 128
WIDTH = 4
GROUP = 256
TOK_DEV = 256
INNER = 4096
E = 4352
SEQUENCE_TOKENS = 2048


def decay_plan(key, fast_share):
    head_key, pick_key = jax.random.split(key, 2)
    coefficient = jnp.exp(jax.random.uniform(head_key, (HEADS,), jnp.float32, 0.0, math.log(8.0)))
    fast = jax.random.uniform(pick_key, (HEADS,), jnp.float32) < fast_share
    target = jnp.where(fast, 1.0 / 40.0, 0.7 / SEQUENCE_TOKENS)
    return (coefficient, target)


def draw_decay_rate(key, part):
    coefficient, target = decay_plan(key, 0.5)
    return coefficient.astype(jnp.float32)


def draw_step_size(key, part):
    coefficient, target = decay_plan(key, 0.5)
    key = jax.random.fold_in(key, 7)
    block_random_key, coarse_random_key, spike_random_key = jax.random.split(key, 3)
    block_factor = jnp.exp(jax.random.uniform(block_random_key, (HEADS, SEQUENCE_TOKENS // TOK_DEV), jnp.float32, math.log(0.5), math.log(2.0)))
    factor = jnp.repeat(block_factor, TOK_DEV, axis=1)
    rough = jax.random.uniform(coarse_random_key, (HEADS, SEQUENCE_TOKENS), jnp.float32, 0.5, 1.5)
    spike_locations = jax.random.randint(spike_random_key, (3,), 0, SEQUENCE_TOKENS)
    spike_train = jnp.any(jnp.arange(SEQUENCE_TOKENS)[:, None] == spike_locations[None, :], axis=1)
    additional_term = jnp.where(spike_train, 0.25, 0.0)
    steps = (target[:, None] * factor * rough + additional_term[None, :]) / coefficient[:, None]
    return steps.astype(jnp.float32)


def steps_of(rng, extent, cuts, low, high):
    gain, own = 1.0, jax.random.fold_in(rng, 6)
    for axis_at, blocks in cuts:
        heights = jnp.exp(jax.random.uniform(jax.random.fold_in(own, axis_at), (blocks,), jnp.float32, low / len(cuts), high / len(cuts)))
        gain = gain * jnp.repeat(heights, extent[axis_at] // blocks).reshape([-1 if axis == axis_at else 1 for axis in range(len(extent))])
    return gain


def bell_draw(stream_key, extent, spread, most, cuts=(), held_as=jnp.bfloat16):
    entries = spread * jax.random.normal(stream_key, extent, jnp.float32)
    if cuts:
        entries = entries * steps_of(stream_key, extent, cuts, -0.22, 0.18)
    return jnp.clip(entries, -most, most).astype(held_as)


def setup_inputs(seed: int = 0, part: int = 0) -> dict:
    key_list = jax.random.split(jax.random.key(seed), 9)
    own_keys = jax.random.split(jax.random.fold_in(key_list[8], part), 9)
    mixer_input = bell_draw(own_keys[0], (SEQUENCE_TOKENS, E), 1.0, 6.0, ((0, 8),))
    gate_input = bell_draw(own_keys[1], (SEQUENCE_TOKENS, INNER), 1.0, 6.0, ((0, 8),))
    conv_forward = bell_draw(key_list[2], (WIDTH, E), WIDTH ** -0.5, 3.0, (), jnp.float32)
    conv_reverse = bell_draw(key_list[3], (WIDTH, E), WIDTH ** -0.5, 3.0, (), jnp.float32)
    step_size = draw_step_size(jax.random.fold_in(jax.random.fold_in(key_list[8], part), 71), part)
    decay_rate = draw_decay_rate(jax.random.fold_in(jax.random.fold_in(key_list[8], part), 71), part)
    skip_scale = jnp.clip(jax.random.uniform(key_list[6], (HEADS,), jnp.float32, 0.5, 1.5), 0.5, 1.5)
    norm_gain = jnp.clip(1.0 + 0.1 * jax.random.normal(key_list[7], (INNER,), jnp.float32), 0.5, 1.5)
    return dict(mixer_input=mixer_input, gate_input=gate_input, conv_forward=conv_forward, conv_reverse=conv_reverse, step_size=step_size, decay_rate=decay_rate, skip_scale=skip_scale, norm_gain=norm_gain)


def conv_pair(padded, conv_forward, conv_reverse, length):
    reach = conv_forward.shape[0] - 1
    ahead = jnp.zeros((length, padded.shape[1]), jnp.float32)
    behind = jnp.zeros((length, padded.shape[1]), jnp.float32)
    for kernel_tap in range(reach + 1):
        ahead = ahead + conv_forward[kernel_tap] * padded[kernel_tap:kernel_tap + length].astype(jnp.float32)
        start = 2 * reach - kernel_tap
        behind = behind + conv_reverse[kernel_tap] * padded[start:start + length].astype(jnp.float32)
    return (jax.nn.silu(ahead).astype(jnp.bfloat16), jax.nn.silu(behind).astype(jnp.bfloat16))

def split_pieces(convolved):
    length = convolved.shape[0]
    inner = HEADS * HEAD_DIM
    values = convolved[:, :inner].reshape(length, HEADS, HEAD_DIM)
    keys = convolved[:, inner:inner + STATE]
    queries = convolved[:, inner + STATE:]
    return (values, keys, queries)

def block_terms(block_values, block_keys, block_queries, block_steps, decay_rate):
    log_steps = -decay_rate[:, None] * block_steps
    cumulative = jnp.cumsum(log_steps, axis=1)
    width = block_steps.shape[1]
    position = jnp.arange(width)
    causal = position[:, None] >= position[None, :]
    segment = jnp.where(causal[None], cumulative[:, :, None] - cumulative[:, None, :], -1e+30)
    intersection = jnp.dot(block_queries, block_keys.T, preferred_element_type=jnp.float32)
    scores = (intersection[None] * jnp.exp(segment) * block_steps[:, None, :]).astype(jnp.bfloat16)
    within = jnp.einsum('hts,shp->thp', scores.astype(jnp.float32), block_values.astype(jnp.float32))
    factors = block_steps * jnp.exp(cumulative[:, -1:] - cumulative)
    weighted = (block_values.astype(jnp.float32) * factors.T[:, :, None]).astype(jnp.bfloat16)
    state = jnp.einsum('tn,thp->hpn', block_keys.astype(jnp.float32), weighted.astype(jnp.float32))
    return (within, state, cumulative)

def directed(values, keys, queries, steps, decay_rate):
    length = values.shape[0]
    block_count = length // GROUP
    value_blocks = values.reshape(block_count, GROUP, HEADS, HEAD_DIM)
    key_blocks = keys.reshape(block_count, GROUP, STATE)
    query_blocks = queries.reshape(block_count, GROUP, STATE)
    step_blocks = steps.reshape(HEADS, block_count, GROUP).transpose(1, 0, 2)

    def advance(carry, item):
        within, state, cumulative = block_terms(item[0], item[1], item[2], item[3], decay_rate)
        carried_term = jnp.einsum('tn,hpn->thp', item[2].astype(jnp.float32), carry, precision=lax.Precision.HIGHEST)
        result = within + jnp.exp(cumulative).T[:, :, None] * carried_term
        carry = jnp.exp(cumulative[:, -1])[:, None, None] * carry + state
        return (carry, result)
    start_state = jnp.zeros((HEADS, HEAD_DIM, STATE), jnp.float32)
    _, results = lax.scan(advance, start_state, (value_blocks, key_blocks, query_blocks, step_blocks))
    return results.reshape(length, HEADS, HEAD_DIM)

def reference(mixer_input, gate_input, conv_forward, conv_reverse, step_size, decay_rate, skip_scale, norm_gain):
    length = mixer_input.shape[0]
    reach = WIDTH - 1
    padded = jnp.pad(mixer_input, ((reach, reach), (0, 0)))
    ahead, behind = conv_pair(padded, conv_forward, conv_reverse, length)
    values_ahead, keys_ahead, queries_ahead = split_pieces(ahead)
    values_behind, keys_behind, queries_behind = split_pieces(behind)
    forward = directed(values_ahead, keys_ahead, queries_ahead, step_size, decay_rate)
    reverse = directed(values_behind[::-1], keys_behind[::-1], queries_behind[::-1], step_size[:, ::-1], decay_rate)[::-1]
    mixed = forward + reverse + skip_scale[None, :, None] * values_ahead.astype(jnp.float32)
    gated = mixed.reshape(length, HEADS * HEAD_DIM) * jax.nn.silu(gate_input.astype(jnp.float32))
    scale = lax.rsqrt(lax.optimization_barrier(jnp.mean(gated * gated, axis=-1, keepdims=True)) + 1e-05)
    return (gated * scale * norm_gain).astype(jnp.bfloat16)
```

```python
import functools

import jax
import jax.numpy as jnp
from jax import lax
from jax.experimental import pallas as pl
from jax.experimental.pallas import tpu as pltpu
from jax.sharding import PartitionSpec as P

HEADS = 64
HEAD_DIM = 64
STATE = 128
WIDTH = 4
BLOCK = 256
INNER = HEADS * HEAD_DIM
PIECE = 256
PIECES = INNER // PIECE
PER = PIECE // HEAD_DIM
HALO = 16
STRIP = 64
LAG = 2
LOG2E = 1.4426950408889634
F32 = jnp.float32
BF16 = jnp.bfloat16
MESH = pl.DeviceIdType.MESH


def dot(a, b):
    return jnp.dot(a, b, preferred_element_type=F32)


def silu(x):
    y = 0.5 * x
    return y + y * jnp.tanh(y)


def kernel(
    n,
    x_hbm, gate_hbm, tapf, tapr, step_ref, decay, skip, gain, out_hbm,
    xpad, gate_v, va, vb, acc, sg, stf, str_, cinf, cinr, sbf, sbr,
    colc, cfs, ces, rowc, aft, sel, drow, gf_ref, gr_ref, kq, kt, ssq, out_v,
    local_sem, halo_send, halo_recv, sendf, recvf, sendr, recvr, out_sem,
):
    me = lax.axis_index("seq")
    has_left = me > 0
    has_right = me < n - 1
    left = lax.rem(me + n - 1, n)
    right = lax.rem(me + 1, n)

    load_x = pltpu.make_async_copy(x_hbm, xpad.at[pl.ds(HALO, BLOCK)], local_sem.at[0])
    load_gate = pltpu.make_async_copy(gate_hbm, gate_v, local_sem.at[1])
    load_x.start()
    load_gate.start()

    barrier = pltpu.get_barrier_semaphore()

    @pl.when(has_left)
    def _():
        pl.semaphore_signal(barrier, inc=1, device_id={"seq": left}, device_id_type=MESH)

    @pl.when(has_right)
    def _():
        pl.semaphore_signal(barrier, inc=1, device_id={"seq": right}, device_id_type=MESH)

    pl.semaphore_wait(barrier, has_left.astype(jnp.int32) + has_right.astype(jnp.int32))

    to_right = pltpu.make_async_remote_copy(
        src_ref=x_hbm.at[pl.ds(BLOCK - HALO, HALO)],
        dst_ref=xpad.at[pl.ds(0, HALO)],
        send_sem=halo_send.at[0],
        recv_sem=halo_recv.at[0],
        device_id={"seq": right},
        device_id_type=MESH,
    )
    to_left = pltpu.make_async_remote_copy(
        src_ref=x_hbm.at[pl.ds(0, HALO)],
        dst_ref=xpad.at[pl.ds(HALO + BLOCK, HALO)],
        send_sem=halo_send.at[1],
        recv_sem=halo_recv.at[1],
        device_id={"seq": left},
        device_id_type=MESH,
    )

    @pl.when(has_right)
    def _():
        to_right.start()

    @pl.when(has_left)
    def _():
        to_left.start()

    @pl.when(jnp.logical_not(has_left))
    def _():
        xpad[0:HALO, :] = jnp.zeros((HALO, xpad.shape[1]), BF16)

    @pl.when(jnp.logical_not(has_right))
    def _():
        xpad[HALO + BLOCK :, :] = jnp.zeros((HALO, xpad.shape[1]), BF16)

    for h in range(HEADS):
        ces[h : h + 1, :] = step_ref[h : h + 1, :] * (decay[h] * -LOG2E)
    logs = ces[...]
    row_i = lax.broadcasted_iota(jnp.int32, (BLOCK, BLOCK), 0)
    col_i = lax.broadcasted_iota(jnp.int32, (BLOCK, BLOCK), 1)
    upto = jnp.where(row_i <= col_i, 1.0, 0.0).astype(F32)
    cum = jnp.dot(logs, upto, preferred_element_type=F32, precision=lax.Precision.HIGHEST)
    before = cum - logs
    total = cum[:, BLOCK - 1 : BLOCK]
    steps = step_ref[...]
    log_steps = jnp.log(steps) * LOG2E
    cfs[...] = cum - log_steps
    ces[...] = before + log_steps
    for p in range(PIECES):
        rowc[p, 0:PER, :] = cfs[p * PER : (p + 1) * PER, :]
        rowc[p, PER : 2 * PER, :] = ces[p * PER : (p + 1) * PER, :]
    columns = jnp.transpose(jnp.concatenate([cum, before], axis=0))
    for p in range(PIECES):
        shift = (STATE - PER * p) % STATE
        colc[p] = pltpu.roll(columns, shift, axis=1) if shift else columns
    factors = (
        steps * jnp.exp2(total - cum),
        steps * jnp.exp2(before),
        jnp.exp2(cum),
        jnp.exp2(total - before),
    )
    parts = []
    for f in factors:
        high = f.astype(BF16).astype(F32)
        parts.append((high, f - high))
    for v in range(PIECES // 4):
        rows = []
        for u in (2 * v, 2 * v + 1):
            for high, low in parts:
                rows.append(high[8 * u : 8 * u + 8])
                rows.append(low[8 * u : 8 * u + 8])
        aft[v] = jnp.transpose(jnp.concatenate(rows, axis=0)).astype(BF16)
    sel_row = lax.broadcasted_iota(jnp.int32, (STATE, PIECE), 0)
    sel_col = lax.broadcasted_iota(jnp.int32, (STATE, PIECE), 1) // HEAD_DIM
    base = sel_row - sel_col
    for q in range(4):
        for f in range(4):
            off = (q // 2) * 64 + f * 16 + (q % 2) * 4
            hit = jnp.logical_or(base == off, base == off + 8)
            sel[q, :, f * PIECE : (f + 1) * PIECE] = jnp.where(hit, 1.0, 0.0).astype(BF16)

    load_x.wait()

    @pl.when(has_right)
    def _():
        to_right.wait_send()
        to_left.wait_recv()

    @pl.when(has_left)
    def _():
        to_right.wait_recv()
        to_left.wait_send()

    def conv(r, cols):
        xs = xpad[pl.ds(r, STRIP + 2 * HALO), cols].astype(F32)
        ahead = behind = None
        rows = STRIP + 2 * HALO

        def at(d):
            moved = xs if d == 0 else pltpu.roll(xs, (-d) % rows, axis=0)
            return moved[HALO : HALO + STRIP]

        fw = tapf[:, cols]
        rv = tapr[:, cols]
        for k in range(WIDTH):
            a = fw[k : k + 1] * at(k - (WIDTH - 1))
            b = rv[k : k + 1] * at(WIDTH - 1 - k)
            ahead = a if ahead is None else ahead + a
            behind = b if behind is None else behind + b
        return silu(ahead).astype(BF16), silu(behind).astype(BF16)

    for which in range(2):
        for r in range(0, BLOCK, STRIP):
            a, b = conv(r, pl.ds(INNER + which * STATE, STATE))
            kq[which, r : r + STRIP, :] = a
            kq[2 + which, r : r + STRIP, :] = b
    kt[0] = jnp.transpose(kq[0].astype(F32)).astype(BF16)
    kt[1] = jnp.transpose(kq[2].astype(F32)).astype(BF16)
    gf_ref[...] = jnp.where(row_i >= col_i, dot(kq[1], kt[0]), 0.0)
    gr_ref[...] = jnp.where(row_i <= col_i, dot(kq[3], kt[1]), 0.0)
    load_gate.wait()

    lane = lax.broadcasted_iota(jnp.int32, (1, STATE), 1)
    first_half = lane < HEAD_DIM

    def make(p):
        v = p // 4
        q = lax.rem(p, 4)
        for c in range(PIECE // STATE):
            cols = pl.ds(pl.multiple_of(p * PIECE + c * STATE, STATE), STATE)
            skip_row = jnp.where(first_half, skip[p * PER + 2 * c], skip[p * PER + 2 * c + 1])
            for r in range(0, BLOCK, STRIP):
                a, b = conv(r, cols)
                here = (p, pl.ds(r, STRIP), pl.ds(c * STATE, STATE))
                va[here] = a
                vb[here] = b
                acc[here] = skip_row * a.astype(F32)
        wide = dot(aft[v], sel[q, :, 0 : 2 * PIECE])
        wf = (va[p].astype(F32) * wide[:, :PIECE]).astype(BF16)
        stf[p] = dot(kt[0], wf)
        wr = (vb[p].astype(F32) * wide[:, PIECE:]).astype(BF16)
        str_[p] = dot(kt[1], wr)
        ends = dot(aft[v, BLOCK - 16 : BLOCK, :], sel[q, :, 2 * PIECE : 3 * PIECE])
        drow[p, 0:1, :] = ends[15:16, :]

    def hop(p, forward):
        cin, sb, st = (cinf, sbf, stf) if forward else (cinr, sbr, str_)
        send, recv = (sendf, recvf) if forward else (sendr, recvr)
        takes, gives = (has_left, has_right) if forward else (has_right, has_left)
        target = right if forward else left
        copy = pltpu.make_async_remote_copy(
            src_ref=sb.at[p],
            dst_ref=cin.at[p],
            send_sem=send.at[p],
            recv_sem=recv.at[p],
            device_id={"seq": target},
            device_id_type=MESH,
        )
        return copy, cin, sb, st, takes, gives

    def chain(p, forward):
        copy, cin, sb, st, takes, gives = hop(p, forward)

        @pl.when(takes)
        def _():
            copy.wait_recv()

            @pl.when(gives)
            def _():
                sb[p] = (st[p] + drow[p, 0:1, :] * cin[p].astype(F32)).astype(BF16)

        @pl.when(jnp.logical_not(takes))
        def _():
            sb[p] = st[p].astype(BF16)

        @pl.when(gives)
        def _():
            copy.start()

        @pl.when(takes)
        def _():
            first = (2 if forward else 3) * PIECE
            grow = dot(aft[p // 4], sel[lax.rem(p, 4), :, first : first + PIECE])
            acc[p] = acc[p] + grow * dot(kq[1 if forward else 3], cin[p])

    half = BLOCK // 2

    def within(p):
        for pair in range(PER // 2):
            lanes = slice(pair * STATE, (pair + 1) * STATE)
            vf = va[p, :, lanes]
            vr = vb[p, :, lanes]
            res = []
            for j in (2 * pair, 2 * pair + 1):
                cft = colc[p, :, j : j + 1]
                cet = colc[p, :, 64 + j : 65 + j]
                ra = rowc[p, j : j + 1, :]
                rb = rowc[p, PER + j : PER + j + 1, :]
                lo, hi = slice(0, half), slice(half, BLOCK)
                d00 = jnp.exp2(jnp.minimum(cft[lo] - ra[:, lo], rb[:, lo] - cet[lo]))
                d01 = jnp.exp2(rb[:, hi] - cet[lo])
                f00 = (gf_ref[lo, lo] * d00).astype(BF16)
                r00 = (gr_ref[lo, lo] * d00).astype(BF16)
                r01 = (gr_ref[lo, hi] * d01).astype(BF16)
                top = dot(f00, vf[lo]) + dot(jnp.concatenate([r00, r01], axis=1), vr)
                d11 = jnp.exp2(jnp.minimum(cft[hi] - ra[:, hi], rb[:, hi] - cet[hi]))
                d10 = jnp.exp2(cft[hi] - ra[:, lo])
                f10 = (gf_ref[hi, lo] * d10).astype(BF16)
                f11 = (gf_ref[hi, hi] * d11).astype(BF16)
                r11 = (gr_ref[hi, hi] * d11).astype(BF16)
                low = dot(jnp.concatenate([f10, f11], axis=1), vf) + dot(r11, vr[hi])
                res.append((top, low))
            for i, rows in enumerate((slice(0, half), slice(half, BLOCK))):
                acc[p, rows, lanes] = acc[p, rows, lanes] + jnp.where(
                    first_half, res[0][i], res[1][i]
                )
        for r in range(0, BLOCK, STRIP):
            g = gate_v[r : r + STRIP, pl.ds(pl.multiple_of(p * PIECE, PIECE), PIECE)]
            sg[p, r : r + STRIP, :] = silu(g.astype(F32))

    def slot(k, carry):
        kf = k - LAG * me
        kr = k - LAG * (n - 1 - me)
        kw = k - PIECES

        @pl.when(k < PIECES)
        def _():
            make(k)

        @pl.when(jnp.logical_and(kf >= 0, kf < PIECES))
        def _():
            chain(kf, True)

        @pl.when(jnp.logical_and(kr >= 0, kr < PIECES))
        def _():
            chain(kr, False)

        @pl.when(jnp.logical_and(kw >= 0, kw < PIECES))
        def _():
            within(kw)

        return carry

    lax.fori_loop(0, PIECES + max(LAG * (n - 1), PIECES), slot, 0)

    ssq[...] = jnp.zeros_like(ssq)

    def gather(p, carry):
        for r in range(0, BLOCK, STRIP):
            rows = pl.ds(r, STRIP)
            y = acc[p, rows, :] * sg[p, rows, :]
            acc[p, rows, :] = y
            y = y * y
            ssq[rows, :] = ssq[rows, :] + (y[:, :STATE] + y[:, STATE:])
        return carry

    lax.fori_loop(0, PIECES, gather, 0)
    scale = lax.rsqrt(jnp.sum(ssq[...], axis=1, keepdims=True) * (1.0 / INNER) + 1e-05)
    ssq[...] = jnp.broadcast_to(scale, ssq.shape)

    copies = []
    for i, r in enumerate(range(0, BLOCK, STRIP)):
        rows = pl.ds(r, STRIP)

        def emit(p, carry):
            cols = pl.ds(pl.multiple_of(p * PIECE, PIECE), PIECE)
            s = ssq[rows, :]
            s = jnp.concatenate([s, s], axis=1)
            out_v[rows, cols] = (acc[p, rows, :] * s * gain[:, cols]).astype(BF16)
            return carry

        lax.fori_loop(0, PIECES, emit, 0)
        copy = pltpu.make_async_copy(out_v.at[rows], out_hbm.at[rows], out_sem.at[i])
        copy.start()
        copies.append(copy)

    @pl.when(has_right)
    def _():
        def done(p, carry):
            hop(p, True)[0].wait_send()
            return carry

        lax.fori_loop(0, PIECES, done, 0)

    @pl.when(has_left)
    def _():
        def done(p, carry):
            hop(p, False)[0].wait_send()
            return carry

        lax.fori_loop(0, PIECES, done, 0)

    for copy in copies:
        copy.wait()


def per_device(
    mixer_input, gate_input, conv_forward, conv_reverse, step_size, decay_rate, skip_scale, norm_gain
):
    n = lax.axis_size("seq")
    vmem = pl.BlockSpec(memory_space=pltpu.VMEM)
    smem = pl.BlockSpec(memory_space=pltpu.SMEM)
    hbm = pl.BlockSpec(memory_space=pl.ANY)
    piece = (PIECES, BLOCK, PIECE)
    state = (PIECES, STATE, PIECE)
    dma = pltpu.SemaphoreType.DMA
    return pl.pallas_call(
        functools.partial(kernel, n),
        out_shape=jax.ShapeDtypeStruct((BLOCK, INNER), BF16),
        in_specs=[hbm, hbm, vmem, vmem, vmem, smem, smem, vmem],
        out_specs=hbm,
        scratch_shapes=[
            pltpu.VMEM((BLOCK + 2 * HALO, INNER + 2 * STATE), BF16),
            pltpu.VMEM((BLOCK, INNER), BF16),
            pltpu.VMEM(piece, BF16),
            pltpu.VMEM(piece, BF16),
            pltpu.VMEM(piece, F32),
            pltpu.VMEM(piece, F32),
            pltpu.VMEM(state, F32),
            pltpu.VMEM(state, F32),
            pltpu.VMEM(state, BF16),
            pltpu.VMEM(state, BF16),
            pltpu.VMEM(state, BF16),
            pltpu.VMEM(state, BF16),
            pltpu.VMEM((PIECES, BLOCK, STATE), F32),
            pltpu.VMEM((HEADS, BLOCK), F32),
            pltpu.VMEM((HEADS, BLOCK), F32),
            pltpu.VMEM((PIECES, 2 * PER, BLOCK), F32),
            pltpu.VMEM((PIECES // 4, BLOCK, STATE), BF16),
            pltpu.VMEM((4, STATE, 4 * PIECE), BF16),
            pltpu.VMEM((PIECES, 8, PIECE), F32),
            pltpu.VMEM((BLOCK, BLOCK), F32),
            pltpu.VMEM((BLOCK, BLOCK), F32),
            pltpu.VMEM((4, BLOCK, STATE), BF16),
            pltpu.VMEM((2, STATE, BLOCK), BF16),
            pltpu.VMEM((BLOCK, STATE), F32),
            pltpu.VMEM((BLOCK, INNER), BF16),
            dma((2,)),
            dma((2,)),
            dma((2,)),
            dma((PIECES,)),
            dma((PIECES,)),
            dma((PIECES,)),
            dma((PIECES,)),
            dma((BLOCK // STRIP,)),
        ],
        compiler_params=pltpu.CompilerParams(
            collective_id=0, has_side_effects=True, vmem_limit_bytes=56 * 1024 * 1024
        ),
        cost_estimate=pl.CostEstimate(flops=3 * 10**9, bytes_accessed=7 * 10**6, transcendentals=10**7),
        name="mixer",
    )(
        mixer_input, gate_input, conv_forward, conv_reverse, step_size, decay_rate, skip_scale,
        norm_gain.reshape(1, INNER),
    )


def solution(mesh):
    in_specs = (
        P(("row", "seq"), None),
        P(("row", "seq"), None),
        P(),
        P(),
        P(None, ("row", "seq")),
        P("row"),
        P(),
        P(),
    )
    out_specs = P(("row", "seq"), None)
    return jax.shard_map(
        per_device, mesh=mesh, in_specs=in_specs, out_specs=out_specs, check_vma=False
    )
```

```python
import functools

import jax
import jax.numpy as jnp
from jax import lax
from jax.experimental import pallas as pl
from jax.experimental.pallas import tpu as pltpu
from jax.sharding import PartitionSpec as P

HEADS = 64
HEAD_DIM = 64
STATE = 128
WIDTH = 4
BLOCK = 256
INNER = HEADS * HEAD_DIM
PIECE = 256
PIECES = INNER // PIECE
PER = PIECE // HEAD_DIM
HALO = 16
STRIP = 64
LAG = 4
LOG2E = 1.4426950408889634
F32 = jnp.float32
BF16 = jnp.bfloat16
MESH = pl.DeviceIdType.MESH


def dot(a, b):
    return jnp.dot(a, b, preferred_element_type=F32)


def silu(x):
    y = 0.5 * x
    return y + y * jnp.tanh(y)


def kernel(
    n,
    x_hbm, gate_hbm, tapf, tapr, step_ref, decay, skip, y_hbm, scale_ref,
    xpad, gate_v, vcat, accw, accf, accr, stf, str_, cinf, cinr, sbf, sbr,
    colc, cfs, ces, rowc, aft, sel, drow, gf_ref, gr_ref, kq, kt, ssq, y_v,
    local_sem, halo_send, halo_recv, sendf, recvf, sendr, recvr, out_sem,
):
    me = lax.axis_index("seq")
    has_left = me > 0
    has_right = me < n - 1
    left = lax.rem(me + n - 1, n)
    right = lax.rem(me + 1, n)

    load_x = pltpu.make_async_copy(x_hbm, xpad.at[pl.ds(HALO, BLOCK)], local_sem.at[0])
    load_gate = pltpu.make_async_copy(gate_hbm, gate_v, local_sem.at[1])
    load_x.start()
    load_gate.start()

    barrier = pltpu.get_barrier_semaphore()

    @pl.when(has_left)
    def _():
        pl.semaphore_signal(barrier, inc=1, device_id={"seq": left}, device_id_type=MESH)

    @pl.when(has_right)
    def _():
        pl.semaphore_signal(barrier, inc=1, device_id={"seq": right}, device_id_type=MESH)

    pl.semaphore_wait(barrier, has_left.astype(jnp.int32) + has_right.astype(jnp.int32))

    to_right = pltpu.make_async_remote_copy(
        src_ref=x_hbm.at[pl.ds(BLOCK - HALO, HALO)],
        dst_ref=xpad.at[pl.ds(0, HALO)],
        send_sem=halo_send.at[0],
        recv_sem=halo_recv.at[0],
        device_id={"seq": right},
        device_id_type=MESH,
    )
    to_left = pltpu.make_async_remote_copy(
        src_ref=x_hbm.at[pl.ds(0, HALO)],
        dst_ref=xpad.at[pl.ds(HALO + BLOCK, HALO)],
        send_sem=halo_send.at[1],
        recv_sem=halo_recv.at[1],
        device_id={"seq": left},
        device_id_type=MESH,
    )

    @pl.when(has_right)
    def _():
        to_right.start()

    @pl.when(has_left)
    def _():
        to_left.start()

    @pl.when(jnp.logical_not(has_left))
    def _():
        xpad[0:HALO, :] = jnp.zeros((HALO, xpad.shape[1]), BF16)

    @pl.when(jnp.logical_not(has_right))
    def _():
        xpad[HALO + BLOCK :, :] = jnp.zeros((HALO, xpad.shape[1]), BF16)

    for h in range(HEADS):
        ces[h : h + 1, :] = step_ref[h : h + 1, :] * (decay[h] * -LOG2E)
    logs = ces[...]
    row_i = lax.broadcasted_iota(jnp.int32, (BLOCK, BLOCK), 0)
    col_i = lax.broadcasted_iota(jnp.int32, (BLOCK, BLOCK), 1)
    upto = jnp.where(row_i <= col_i, 1.0, 0.0).astype(F32)
    cum = jnp.dot(logs, upto, preferred_element_type=F32, precision=lax.Precision.HIGHEST)
    before = cum - logs
    total = cum[:, BLOCK - 1 : BLOCK]
    steps = step_ref[...]
    log_steps = jnp.log(steps) * LOG2E
    cfs[...] = cum - log_steps
    ces[...] = before + log_steps
    for p in range(PIECES):
        rowc[p, 0:PER, :] = cfs[p * PER : (p + 1) * PER, :]
        rowc[p, PER : 2 * PER, :] = ces[p * PER : (p + 1) * PER, :]
    columns = jnp.transpose(jnp.concatenate([cum, before], axis=0))
    for p in range(PIECES):
        shift = (STATE - PER * p) % STATE
        colc[p] = pltpu.roll(columns, shift, axis=1) if shift else columns
    factors = (
        steps * jnp.exp2(total - cum),
        steps * jnp.exp2(before),
        jnp.exp2(cum),
        jnp.exp2(total - before),
    )
    parts = []
    for f in factors:
        high = f.astype(BF16).astype(F32)
        parts.append((high, f - high))
    for v in range(PIECES // 4):
        rows = []
        for u in (2 * v, 2 * v + 1):
            for high, low in parts:
                rows.append(high[8 * u : 8 * u + 8])
                rows.append(low[8 * u : 8 * u + 8])
        aft[v] = jnp.transpose(jnp.concatenate(rows, axis=0)).astype(BF16)
    sel_row = lax.broadcasted_iota(jnp.int32, (STATE, PIECE), 0)
    sel_col = lax.broadcasted_iota(jnp.int32, (STATE, PIECE), 1) // HEAD_DIM
    base = sel_row - sel_col
    for q in range(4):
        for f in range(4):
            off = (q // 2) * 64 + f * 16 + (q % 2) * 4
            hit = jnp.logical_or(base == off, base == off + 8)
            sel[q, :, f * PIECE : (f + 1) * PIECE] = jnp.where(hit, 1.0, 0.0).astype(BF16)

    half = BLOCK // 2
    load_x.wait()

    @pl.when(has_right)
    def _():
        to_right.wait_send()
        to_left.wait_recv()

    @pl.when(has_left)
    def _():
        to_right.wait_recv()
        to_left.wait_send()

    def conv(r, cols):
        xs = xpad[pl.ds(r, STRIP + 2 * HALO), cols].astype(F32)[8 : STRIP + 24]
        ahead = behind = None
        rows = STRIP + 16

        def at(d):
            moved = xs if d == 0 else pltpu.roll(xs, (-d) % rows, axis=0)
            return moved[8 : 8 + STRIP]

        fw = tapf[:, cols]
        rv = tapr[:, cols]
        for k in range(WIDTH):
            a = fw[k : k + 1] * at(k - (WIDTH - 1))
            b = rv[k : k + 1] * at(WIDTH - 1 - k)
            ahead = a if ahead is None else ahead + a
            behind = b if behind is None else behind + b
        return silu(ahead).astype(BF16), silu(behind).astype(BF16)

    for which in range(2):
        for r in range(0, BLOCK, STRIP):
            a, b = conv(r, pl.ds(INNER + which * STATE, STATE))
            kq[which, r : r + STRIP, :] = a
            kq[2 + which, r : r + STRIP, :] = b
    lo, hi = slice(0, half), slice(half, BLOCK)
    for i in range(2):
        keys = jnp.transpose(kq[2 * i].astype(F32)).astype(BF16)
        kt[i, :, lo] = keys[:, hi]
        kt[i, :, hi] = keys[:, lo]
        inside = row_i >= col_i if i == 0 else row_i <= col_i
        (gf_ref, gr_ref)[i][...] = jnp.where(inside, dot(kq[2 * i + 1], keys), 0.0)
    load_gate.wait()

    lane = lax.broadcasted_iota(jnp.int32, (1, STATE), 1)
    first_half = lane < HEAD_DIM

    def make(p):
        v = p // 4
        q = lax.rem(p, 4)
        for c in range(PIECE // STATE):
            cols = pl.ds(pl.multiple_of(p * PIECE + c * STATE, STATE), STATE)
            for r in range(0, BLOCK, STRIP):
                a, b = conv(r, cols)
                at = (r + half) % BLOCK
                vcat[p, pl.ds(at, STRIP), pl.ds(c * STATE, STATE)] = a
                vcat[p, pl.ds(BLOCK + at, STRIP), pl.ds(c * STATE, STATE)] = b
        ends = dot(aft[v, BLOCK - 16 : BLOCK, :], sel[q, :, 2 * PIECE : 3 * PIECE])
        drow[p, 0:1, :] = ends[15:16, :]
        for i, (st, sb, first, gives) in enumerate(
            (
                (stf, sbf, jnp.logical_not(has_left), has_right),
                (str_, sbr, jnp.logical_not(has_right), has_left),
            )
        ):
            wide = dot(aft[v], sel[q, :, i * PIECE : (i + 1) * PIECE])
            top = i * BLOCK
            w = jnp.concatenate(
                [
                    (vcat[p, top : top + half, :].astype(F32) * wide[hi]).astype(BF16),
                    (vcat[p, top + half : top + BLOCK, :].astype(F32) * wide[lo]).astype(BF16),
                ],
                axis=0,
            )
            state = dot(kt[i], w)
            st[p] = state

            @pl.when(first)
            def _():
                sb[p] = state.astype(BF16)
                hop(p, i == 0)[0].start()

    def hop(p, forward):
        cin, sb, st = (cinf, sbf, stf) if forward else (cinr, sbr, str_)
        send, recv = (sendf, recvf) if forward else (sendr, recvr)
        takes, gives = (has_left, has_right) if forward else (has_right, has_left)
        target = right if forward else left
        copy = pltpu.make_async_remote_copy(
            src_ref=sb.at[p],
            dst_ref=cin.at[p],
            send_sem=send.at[p],
            recv_sem=recv.at[p],
            device_id={"seq": target},
            device_id_type=MESH,
        )
        return copy, cin, sb, st, takes, gives

    def relay(p, forward):
        copy, cin, sb, st, takes, gives = hop(p, forward)

        @pl.when(takes)
        def _():
            copy.wait_recv()

            @pl.when(gives)
            def _():
                sb[p] = (st[p] + drow[p, 0:1, :] * cin[p].astype(F32)).astype(BF16)
                copy.start()

    def enter(p, forward):
        cin, acc = (cinf, accf) if forward else (cinr, accr)
        takes = has_left if forward else has_right

        @pl.when(takes)
        def _():
            first = (2 if forward else 3) * PIECE
            grow = dot(aft[p // 4], sel[lax.rem(p, 4), :, first : first + PIECE])
            acc[p] = grow * dot(kq[1 if forward else 3], cin[p])

        @pl.when(jnp.logical_not(takes))
        def _():
            acc[p] = jnp.zeros((BLOCK, PIECE), F32)

    def within(p):
        for pair in range(PER // 2):
            lanes = slice(pair * STATE, (pair + 1) * STATE)
            tops, lows = [], []
            for j in (2 * pair, 2 * pair + 1):
                cft = colc[p, :, j : j + 1]
                cet = colc[p, :, 64 + j : 65 + j]
                ra = rowc[p, j : j + 1, :]
                rb = rowc[p, PER + j : PER + j + 1, :]
                d00 = jnp.exp2(jnp.minimum(cft[lo] - ra[:, lo], rb[:, lo] - cet[lo]))
                f00 = (gf_ref[lo, lo] * d00).astype(BF16)
                r00 = (gr_ref[lo, lo] * d00).astype(BF16)
                d01 = jnp.exp2(rb[:, hi] - cet[lo])
                r01 = (gr_ref[lo, hi] * d01).astype(BF16)
                tops.append(jnp.concatenate([f00, r01, r00], axis=1))
                d11 = jnp.exp2(jnp.minimum(cft[hi] - ra[:, hi], rb[:, hi] - cet[hi]))
                f11 = (gf_ref[hi, hi] * d11).astype(BF16)
                r11 = (gr_ref[hi, hi] * d11).astype(BF16)
                d10 = jnp.exp2(cft[hi] - ra[:, lo])
                f10 = (gf_ref[hi, lo] * d10).astype(BF16)
                lows.append(jnp.concatenate([f11, f10, r11], axis=1))
            top = dot(jnp.concatenate(tops, axis=0), vcat[p, half : 2 * BLOCK, lanes])
            low = dot(jnp.concatenate(lows, axis=0), vcat[p, 0 : BLOCK + half, lanes])
            skip_row = jnp.where(first_half, skip[p * PER + 2 * pair], skip[p * PER + 2 * pair + 1])
            for rows, res, at in ((lo, top, half), (hi, low, 0)):
                direct = skip_row * vcat[p, at : at + half, lanes].astype(F32)
                accw[p, rows, lanes] = direct + jnp.where(first_half, res[:half], res[half:])

    def y_copy(p):
        cols = pl.ds(pl.multiple_of(p * PIECE, PIECE), PIECE)
        return pltpu.make_async_copy(y_v.at[p], y_hbm.at[:, cols], out_sem.at[p])

    def gather(p):
        cols = pl.ds(pl.multiple_of(p * PIECE, PIECE), PIECE)
        for r in range(0, BLOCK, STRIP):
            rows = pl.ds(r, STRIP)
            gate = silu(gate_v[rows, cols].astype(F32))
            y = (accw[p, rows, :] + (accf[p, rows, :] + accr[p, rows, :])) * gate
            y_v[p, rows, :] = y.astype(BF16)
            y = y * y
            ssq[rows, :] = ssq[rows, :] + (y[:, :STATE] + y[:, STATE:])
        y_copy(p).start()

    ssq[...] = jnp.zeros_like(ssq)
    behind_f = LAG * me
    behind_r = LAG * (n - 1 - me)
    behind_w = PIECES
    behind_y = jnp.maximum(jnp.maximum(behind_f, behind_r), behind_w)

    def slot(k, carry):
        def step(late, work):
            p = k - late

            @pl.when(jnp.logical_and(p >= 0, p < PIECES))
            def _():
                work(p)

        step(behind_f, lambda p: relay(p, True))
        step(behind_r, lambda p: relay(p, False))
        step(0, make)
        step(behind_w, within)
        step(behind_f, lambda p: enter(p, True))
        step(behind_r, lambda p: enter(p, False))
        step(behind_y, gather)
        return carry

    lax.fori_loop(0, PIECES + max(LAG * (n - 1), PIECES), slot, 0)
    mean = jnp.sum(ssq[...], axis=1, keepdims=True) * (1.0 / INNER)
    scale_ref[...] = jnp.broadcast_to(lax.rsqrt(mean + 1e-05), scale_ref.shape)

    @pl.when(has_right)
    def _():
        def done(p, carry):
            hop(p, True)[0].wait_send()
            return carry

        lax.fori_loop(0, PIECES, done, 0)

    @pl.when(has_left)
    def _():
        def done(p, carry):
            hop(p, False)[0].wait_send()
            return carry

        lax.fori_loop(0, PIECES, done, 0)

    def stored(p, carry):
        y_copy(p).wait()
        return carry

    lax.fori_loop(0, PIECES, stored, 0)


def per_device(
    mixer_input, gate_input, conv_forward, conv_reverse, step_size, decay_rate, skip_scale, norm_gain
):
    n = lax.axis_size("seq")
    vmem = pl.BlockSpec(memory_space=pltpu.VMEM)
    smem = pl.BlockSpec(memory_space=pltpu.SMEM)
    hbm = pl.BlockSpec(memory_space=pl.ANY)
    piece = (PIECES, BLOCK, PIECE)
    state = (PIECES, STATE, PIECE)
    dma = pltpu.SemaphoreType.DMA
    y, scale = pl.pallas_call(
        functools.partial(kernel, n),
        out_shape=(
            jax.ShapeDtypeStruct((BLOCK, INNER), BF16),
            jax.ShapeDtypeStruct((BLOCK, STATE), F32),
        ),
        in_specs=[hbm, hbm, vmem, vmem, vmem, smem, smem],
        out_specs=(hbm, vmem),
        scratch_shapes=[
            pltpu.VMEM((BLOCK + 2 * HALO, INNER + 2 * STATE), BF16),
            pltpu.VMEM((BLOCK, INNER), BF16),
            pltpu.VMEM((PIECES, 2 * BLOCK, PIECE), BF16),
            pltpu.VMEM(piece, F32),
            pltpu.VMEM(piece, F32),
            pltpu.VMEM(piece, F32),
            pltpu.VMEM(state, F32),
            pltpu.VMEM(state, F32),
            pltpu.VMEM(state, BF16),
            pltpu.VMEM(state, BF16),
            pltpu.VMEM(state, BF16),
            pltpu.VMEM(state, BF16),
            pltpu.VMEM((PIECES, BLOCK, STATE), F32),
            pltpu.VMEM((HEADS, BLOCK), F32),
            pltpu.VMEM((HEADS, BLOCK), F32),
            pltpu.VMEM((PIECES, 2 * PER, BLOCK), F32),
            pltpu.VMEM((PIECES // 4, BLOCK, STATE), BF16),
            pltpu.VMEM((4, STATE, 4 * PIECE), BF16),
            pltpu.VMEM((PIECES, 8, PIECE), F32),
            pltpu.VMEM((BLOCK, BLOCK), F32),
            pltpu.VMEM((BLOCK, BLOCK), F32),
            pltpu.VMEM((4, BLOCK, STATE), BF16),
            pltpu.VMEM((2, STATE, BLOCK), BF16),
            pltpu.VMEM((BLOCK, STATE), F32),
            pltpu.VMEM(piece, BF16),
            dma((2,)),
            dma((2,)),
            dma((2,)),
            dma((PIECES,)),
            dma((PIECES,)),
            dma((PIECES,)),
            dma((PIECES,)),
            dma((PIECES,)),
        ],
        compiler_params=pltpu.CompilerParams(
            collective_id=0, has_side_effects=True, vmem_limit_bytes=56 * 1024 * 1024
        ),
        cost_estimate=pl.CostEstimate(flops=3 * 10**9, bytes_accessed=7 * 10**6, transcendentals=10**7),
        name="mixer",
    )(
        mixer_input, gate_input, conv_forward, conv_reverse, step_size, decay_rate, skip_scale
    )
    return (y.astype(F32) * scale[:, :1] * norm_gain).astype(BF16)


def solution(mesh):
    in_specs = (
        P(("row", "seq"), None),
        P(("row", "seq"), None),
        P(),
        P(),
        P(None, ("row", "seq")),
        P("row"),
        P(),
        P(),
    )
    out_specs = P(("row", "seq"), None)
    return jax.shard_map(
        per_device, mesh=mesh, in_specs=in_specs, out_specs=out_specs, check_vma=False
    )
```

```python
import functools

import jax
import jax.numpy as jnp
from jax import lax
from jax.experimental import pallas as pl
from jax.experimental.pallas import tpu as pltpu
from jax.sharding import PartitionSpec as P

HEADS = 64
HEAD_DIM = 64
STATE = 128
WIDTH = 4
BLOCK = 256
INNER = HEADS * HEAD_DIM
PIECE = 256
PIECES = INNER // PIECE
PER = PIECE // HEAD_DIM
HALO = 16
STRIP = 64
LAG = 2
LOG2E = 1.4426950408889634
F32 = jnp.float32
BF16 = jnp.bfloat16
MESH = pl.DeviceIdType.MESH


def dot(a, b):
    return jnp.dot(a, b, preferred_element_type=F32)


def silu(x):
    y = 0.5 * x
    return y + y * jnp.tanh(y)


def kernel(
    n,
    x_hbm, gate_hbm, tapf, tapr, step_ref, decay, skip, y_hbm, scale_ref,
    xpad, gate_v, vcat, accw, stf, str_, cinf, cinr, sbf, sbr,
    colc, cfs, ces, rowc, aft, sel, drow, gf_ref, gr_ref, kq, kt, ssq, y_v,
    local_sem, halo_send, halo_recv, sendf, recvf, sendr, recvr, out_sem,
):
    me = lax.axis_index("seq")
    has_left = me > 0
    has_right = me < n - 1
    left = lax.rem(me + n - 1, n)
    right = lax.rem(me + 1, n)

    load_x = pltpu.make_async_copy(x_hbm, xpad.at[pl.ds(HALO, BLOCK)], local_sem.at[0])
    load_gate = pltpu.make_async_copy(gate_hbm, gate_v, local_sem.at[1])
    load_x.start()
    load_gate.start()

    barrier = pltpu.get_barrier_semaphore()

    @pl.when(has_left)
    def _():
        pl.semaphore_signal(barrier, inc=1, device_id={"seq": left}, device_id_type=MESH)

    @pl.when(has_right)
    def _():
        pl.semaphore_signal(barrier, inc=1, device_id={"seq": right}, device_id_type=MESH)

    pl.semaphore_wait(barrier, has_left.astype(jnp.int32) + has_right.astype(jnp.int32))

    to_right = pltpu.make_async_remote_copy(
        src_ref=x_hbm.at[pl.ds(BLOCK - HALO, HALO)],
        dst_ref=xpad.at[pl.ds(0, HALO)],
        send_sem=halo_send.at[0],
        recv_sem=halo_recv.at[0],
        device_id={"seq": right},
        device_id_type=MESH,
    )
    to_left = pltpu.make_async_remote_copy(
        src_ref=x_hbm.at[pl.ds(0, HALO)],
        dst_ref=xpad.at[pl.ds(HALO + BLOCK, HALO)],
        send_sem=halo_send.at[1],
        recv_sem=halo_recv.at[1],
        device_id={"seq": left},
        device_id_type=MESH,
    )

    @pl.when(has_right)
    def _():
        to_right.start()

    @pl.when(has_left)
    def _():
        to_left.start()

    @pl.when(jnp.logical_not(has_left))
    def _():
        cinf[...] = jnp.zeros(cinf.shape, BF16)
        xpad[0:HALO, :] = jnp.zeros((HALO, xpad.shape[1]), BF16)

    @pl.when(jnp.logical_not(has_right))
    def _():
        cinr[...] = jnp.zeros(cinr.shape, BF16)
        xpad[HALO + BLOCK :, :] = jnp.zeros((HALO, xpad.shape[1]), BF16)

    for h in range(HEADS):
        ces[h : h + 1, :] = step_ref[h : h + 1, :] * (decay[h] * -LOG2E)
    logs = ces[...]
    row_i = lax.broadcasted_iota(jnp.int32, (BLOCK, BLOCK), 0)
    col_i = lax.broadcasted_iota(jnp.int32, (BLOCK, BLOCK), 1)
    upto = jnp.where(row_i <= col_i, 1.0, 0.0).astype(F32)
    cum = jnp.dot(logs, upto, preferred_element_type=F32, precision=lax.Precision.HIGHEST)
    before = cum - logs
    total = cum[:, BLOCK - 1 : BLOCK]
    steps = step_ref[...]
    log_steps = jnp.log(steps) * LOG2E
    cfs[...] = cum - log_steps
    ces[...] = before + log_steps
    for p in range(PIECES):
        rowc[p, 0:PER, :] = cfs[p * PER : (p + 1) * PER, :]
        rowc[p, PER : 2 * PER, :] = ces[p * PER : (p + 1) * PER, :]
    columns = jnp.transpose(jnp.concatenate([cum, before], axis=0))
    for p in range(PIECES):
        shift = (STATE - PER * p) % STATE
        colc[p] = pltpu.roll(columns, shift, axis=1) if shift else columns
    factors = (
        steps * jnp.exp2(total - cum),
        steps * jnp.exp2(before),
        jnp.exp2(cum),
        jnp.exp2(total - before),
    )
    parts = []
    for f in factors:
        high = f.astype(BF16).astype(F32)
        parts.append((high, f - high))
    for v in range(PIECES // 4):
        rows = []
        for u in (2 * v, 2 * v + 1):
            for high, low in parts:
                rows.append(high[8 * u : 8 * u + 8])
                rows.append(low[8 * u : 8 * u + 8])
        aft[v] = jnp.transpose(jnp.concatenate(rows, axis=0)).astype(BF16)
    sel_row = lax.broadcasted_iota(jnp.int32, (STATE, PIECE), 0)
    sel_col = lax.broadcasted_iota(jnp.int32, (STATE, PIECE), 1) // HEAD_DIM
    base = sel_row - sel_col
    for q in range(4):
        for f in range(4):
            off = (q // 2) * 64 + f * 16 + (q % 2) * 4
            hit = jnp.logical_or(base == off, base == off + 8)
            sel[q, :, f * PIECE : (f + 1) * PIECE] = jnp.where(hit, 1.0, 0.0).astype(BF16)

    half = BLOCK // 2
    load_x.wait()

    @pl.when(has_right)
    def _():
        to_right.wait_send()
        to_left.wait_recv()

    @pl.when(has_left)
    def _():
        to_right.wait_recv()
        to_left.wait_send()

    def conv(r, cols):
        xs = xpad[pl.ds(r, STRIP + 2 * HALO), cols].astype(F32)[8 : STRIP + 24]
        ahead = behind = None
        rows = STRIP + 16

        def at(d):
            moved = xs if d == 0 else pltpu.roll(xs, (-d) % rows, axis=0)
            return moved[8 : 8 + STRIP]

        fw = tapf[:, cols]
        rv = tapr[:, cols]
        for k in range(WIDTH):
            a = fw[k : k + 1] * at(k - (WIDTH - 1))
            b = rv[k : k + 1] * at(WIDTH - 1 - k)
            ahead = a if ahead is None else ahead + a
            behind = b if behind is None else behind + b
        return silu(ahead).astype(BF16), silu(behind).astype(BF16)

    for which in range(2):
        for r in range(0, BLOCK, STRIP):
            a, b = conv(r, pl.ds(INNER + which * STATE, STATE))
            kq[which, r : r + STRIP, :] = a
            kq[2 + which, r : r + STRIP, :] = b
    lo, hi = slice(0, half), slice(half, BLOCK)
    for i in range(2):
        keys = jnp.transpose(kq[2 * i].astype(F32)).astype(BF16)
        kt[i, :, lo] = keys[:, hi]
        kt[i, :, hi] = keys[:, lo]
        inside = row_i >= col_i if i == 0 else row_i <= col_i
        (gf_ref, gr_ref)[i][...] = jnp.where(inside, dot(kq[2 * i + 1], keys), 0.0)
    load_gate.wait()

    lane = lax.broadcasted_iota(jnp.int32, (1, STATE), 1)
    first_half = lane < HEAD_DIM

    def convolve(p):
        for c in range(PIECE // STATE):
            cols = pl.ds(pl.multiple_of(p * PIECE + c * STATE, STATE), STATE)
            for r in range(0, BLOCK, STRIP):
                a, b = conv(r, cols)
                at = (r + half) % BLOCK
                vcat[p, pl.ds(at, STRIP), pl.ds(c * STATE, STATE)] = a
                vcat[p, pl.ds(BLOCK + at, STRIP), pl.ds(c * STATE, STATE)] = b

    def states(p):
        v = p // 4
        q = lax.rem(p, 4)
        ends = dot(aft[v, BLOCK - 16 : BLOCK, :], sel[q, :, 2 * PIECE : 3 * PIECE])
        drow[p, 0:1, :] = ends[15:16, :]
        for i, st in enumerate((stf, str_)):
            wide = dot(aft[v], sel[q, :, i * PIECE : (i + 1) * PIECE])
            top = i * BLOCK
            w = jnp.concatenate(
                [
                    (vcat[p, top : top + half, :].astype(F32) * wide[hi]).astype(BF16),
                    (vcat[p, top + half : top + BLOCK, :].astype(F32) * wide[lo]).astype(BF16),
                ],
                axis=0,
            )
            st[p] = dot(kt[i], w)

    def hop(p, forward):
        sb, cin = (sbf, cinf) if forward else (sbr, cinr)
        send, recv = (sendf, recvf) if forward else (sendr, recvr)
        return pltpu.make_async_remote_copy(
            src_ref=sb.at[p],
            dst_ref=cin.at[p],
            send_sem=send.at[p],
            recv_sem=recv.at[p],
            device_id={"seq": right if forward else left},
            device_id_type=MESH,
        )

    def relay(p, forward):
        copy = hop(p, forward)
        cin, sb, st = (cinf, sbf, stf) if forward else (cinr, sbr, str_)
        takes, gives = (has_left, has_right) if forward else (has_right, has_left)

        @pl.when(takes)
        def _():
            copy.wait_recv()

        @pl.when(gives)
        def _():
            sb[p] = (st[p] + drow[p, 0:1, :] * cin[p].astype(F32)).astype(BF16)
            copy.start()

    def within(p):
        for pair in range(PER // 2):
            lanes = slice(pair * STATE, (pair + 1) * STATE)
            tops, lows = [], []
            for j in (2 * pair, 2 * pair + 1):
                cft = colc[p, :, j : j + 1]
                cet = colc[p, :, 64 + j : 65 + j]
                ra = rowc[p, j : j + 1, :]
                rb = rowc[p, PER + j : PER + j + 1, :]
                d00 = jnp.exp2(jnp.minimum(cft[lo] - ra[:, lo], rb[:, lo] - cet[lo]))
                f00 = (gf_ref[lo, lo] * d00).astype(BF16)
                r00 = (gr_ref[lo, lo] * d00).astype(BF16)
                d01 = jnp.exp2(rb[:, hi] - cet[lo])
                r01 = (gr_ref[lo, hi] * d01).astype(BF16)
                tops.append(jnp.concatenate([f00, r01, r00], axis=1))
                d11 = jnp.exp2(jnp.minimum(cft[hi] - ra[:, hi], rb[:, hi] - cet[hi]))
                f11 = (gf_ref[hi, hi] * d11).astype(BF16)
                r11 = (gr_ref[hi, hi] * d11).astype(BF16)
                d10 = jnp.exp2(cft[hi] - ra[:, lo])
                f10 = (gf_ref[hi, lo] * d10).astype(BF16)
                lows.append(jnp.concatenate([f11, f10, r11], axis=1))
            top = dot(jnp.concatenate(tops, axis=0), vcat[p, half : 2 * BLOCK, lanes])
            low = dot(jnp.concatenate(lows, axis=0), vcat[p, 0 : BLOCK + half, lanes])
            skip_row = jnp.where(first_half, skip[p * PER + 2 * pair], skip[p * PER + 2 * pair + 1])
            for rows, res, at in ((lo, top, half), (hi, low, 0)):
                direct = skip_row * vcat[p, at : at + half, lanes].astype(F32)
                accw[p, rows, lanes] = direct + jnp.where(first_half, res[:half], res[half:])

    def y_copy(p):
        cols = pl.ds(pl.multiple_of(p * PIECE, PIECE), PIECE)
        return pltpu.make_async_copy(y_v.at[p], y_hbm.at[:, cols], out_sem.at[p])

    def finish(p):
        v = p // 4
        q = lax.rem(p, 4)
        cols = pl.ds(pl.multiple_of(p * PIECE, PIECE), PIECE)
        growf = dot(aft[v], sel[q, :, 2 * PIECE : 3 * PIECE])
        growr = dot(aft[v], sel[q, :, 3 * PIECE : 4 * PIECE])
        f = dot(kq[1], cinf[p])
        r = dot(kq[3], cinr[p])
        gate = silu(gate_v[:, cols].astype(F32))
        y = (accw[p] + (growf * f + growr * r)) * gate
        y_v[p] = y.astype(BF16)
        y = y * y
        ssq[...] = ssq[...] + (y[:, :STATE] + y[:, STATE:])
        y_copy(p).start()

    ssq[...] = jnp.zeros_like(ssq)
    second = 1 + max(PIECES, LAG * (n - 1))

    def relays(k):
        for forward, late in ((True, 1 + LAG * me), (False, 1 + LAG * (n - 1 - me))):
            p = k - late

            @pl.when(jnp.logical_and(p >= 0, p < PIECES))
            def _():
                relay(p, forward)

    convolve(0)

    def slot_a(k, carry):
        states(k - 1)
        convolve(k)
        relays(k)
        return carry

    lax.fori_loop(1, PIECES, slot_a, 0)
    states(PIECES - 1)

    def slot_idle(k, carry):
        relays(k)
        return carry

    lax.fori_loop(PIECES, second, slot_idle, 0)
    relays(second)
    within(0)

    def slot_b(k, carry):
        relays(k)
        finish(k - second - 1)
        within(k - second)
        return carry

    lax.fori_loop(second + 1, second + PIECES, slot_b, 0)
    finish(PIECES - 1)
    mean = jnp.sum(ssq[...], axis=1, keepdims=True) * (1.0 / INNER)
    scale_ref[...] = jnp.broadcast_to(lax.rsqrt(mean + 1e-05), scale_ref.shape)

    @pl.when(has_right)
    def _():
        def done(p, carry):
            hop(p, True).wait_send()
            return carry

        lax.fori_loop(0, PIECES, done, 0)

    @pl.when(has_left)
    def _():
        def done(p, carry):
            hop(p, False).wait_send()
            return carry

        lax.fori_loop(0, PIECES, done, 0)

    def stored(p, carry):
        y_copy(p).wait()
        return carry

    lax.fori_loop(0, PIECES, stored, 0)


def scale_rows(y_hbm, scale_ref, gain_ref, out_hbm, y_v, out_v, in_sem, out_sem):
    parts = [pl.ds(r, STRIP) for r in range(0, BLOCK, STRIP)]
    loads = [pltpu.make_async_copy(y_hbm.at[s], y_v.at[s], in_sem.at[i]) for i, s in enumerate(parts)]
    stores = [
        pltpu.make_async_copy(out_v.at[s], out_hbm.at[s], out_sem.at[i]) for i, s in enumerate(parts)
    ]
    for load in loads:
        load.start()
    for i, rows in enumerate(parts):
        loads[i].wait()
        scale = scale_ref[rows, :]
        for c in range(0, INNER, STATE):
            cols = pl.ds(c, STATE)
            out_v[rows, cols] = (y_v[rows, cols].astype(F32) * scale * gain_ref[:, cols]).astype(BF16)
        stores[i].start()
    for store in stores:
        store.wait()


def per_device(
    mixer_input, gate_input, conv_forward, conv_reverse, step_size, decay_rate, skip_scale, norm_gain
):
    n = lax.axis_size("seq")
    vmem = pl.BlockSpec(memory_space=pltpu.VMEM)
    smem = pl.BlockSpec(memory_space=pltpu.SMEM)
    hbm = pl.BlockSpec(memory_space=pl.ANY)
    piece = (PIECES, BLOCK, PIECE)
    state = (PIECES, STATE, PIECE)
    dma = pltpu.SemaphoreType.DMA
    y, scale = pl.pallas_call(
        functools.partial(kernel, n),
        out_shape=(
            jax.ShapeDtypeStruct((BLOCK, INNER), BF16),
            jax.ShapeDtypeStruct((BLOCK, STATE), F32),
        ),
        in_specs=[hbm, hbm, vmem, vmem, vmem, smem, smem],
        out_specs=(hbm, vmem),
        scratch_shapes=[
            pltpu.VMEM((BLOCK + 2 * HALO, INNER + 2 * STATE), BF16),
            pltpu.VMEM((BLOCK, INNER), BF16),
            pltpu.VMEM((PIECES, 2 * BLOCK, PIECE), BF16),
            pltpu.VMEM(piece, F32),
            pltpu.VMEM(state, F32),
            pltpu.VMEM(state, F32),
            pltpu.VMEM(state, BF16),
            pltpu.VMEM(state, BF16),
            pltpu.VMEM(state, BF16),
            pltpu.VMEM(state, BF16),
            pltpu.VMEM((PIECES, BLOCK, STATE), F32),
            pltpu.VMEM((HEADS, BLOCK), F32),
            pltpu.VMEM((HEADS, BLOCK), F32),
            pltpu.VMEM((PIECES, 2 * PER, BLOCK), F32),
            pltpu.VMEM((PIECES // 4, BLOCK, STATE), BF16),
            pltpu.VMEM((4, STATE, 4 * PIECE), BF16),
            pltpu.VMEM((PIECES, 8, PIECE), F32),
            pltpu.VMEM((BLOCK, BLOCK), F32),
            pltpu.VMEM((BLOCK, BLOCK), F32),
            pltpu.VMEM((4, BLOCK, STATE), BF16),
            pltpu.VMEM((2, STATE, BLOCK), BF16),
            pltpu.VMEM((BLOCK, STATE), F32),
            pltpu.VMEM(piece, BF16),
            dma((2,)),
            dma((2,)),
            dma((2,)),
            dma((PIECES,)),
            dma((PIECES,)),
            dma((PIECES,)),
            dma((PIECES,)),
            dma((PIECES,)),
        ],
        compiler_params=pltpu.CompilerParams(
            collective_id=0, has_side_effects=True, vmem_limit_bytes=56 * 1024 * 1024
        ),
        cost_estimate=pl.CostEstimate(flops=3 * 10**9, bytes_accessed=7 * 10**6, transcendentals=10**7),
        name="mixer",
    )(
        mixer_input, gate_input, conv_forward, conv_reverse, step_size, decay_rate, skip_scale
    )
    dma = pltpu.SemaphoreType.DMA
    parts = BLOCK // STRIP
    return pl.pallas_call(
        scale_rows,
        out_shape=jax.ShapeDtypeStruct((BLOCK, INNER), BF16),
        in_specs=[hbm, vmem, vmem],
        out_specs=hbm,
        scratch_shapes=[
            pltpu.VMEM((BLOCK, INNER), BF16),
            pltpu.VMEM((BLOCK, INNER), BF16),
            dma((parts,)),
            dma((parts,)),
        ],
        compiler_params=pltpu.CompilerParams(vmem_limit_bytes=32 * 1024 * 1024),
        cost_estimate=pl.CostEstimate(flops=2 * 10**6, bytes_accessed=4 * 10**6, transcendentals=0),
        name="scale_rows",
    )(y, scale, norm_gain.reshape(1, INNER))


def solution(mesh):
    in_specs = (
        P(("row", "seq"), None),
        P(("row", "seq"), None),
        P(),
        P(),
        P(None, ("row", "seq")),
        P("row"),
        P(),
        P(),
    )
    out_specs = P(("row", "seq"), None)
    return jax.shard_map(
        per_device, mesh=mesh, in_specs=in_specs, out_specs=out_specs, check_vma=False
    )
```

```python
import functools

import jax
import jax.numpy as jnp
from jax import lax
from jax.experimental import pallas as pl
from jax.experimental.pallas import tpu as pltpu
from jax.sharding import PartitionSpec as P

HEADS = 64
HEAD_DIM = 64
STATE = 128
WIDTH = 4
BLOCK = 256
INNER = HEADS * HEAD_DIM
PIECE = 256
PIECES = INNER // PIECE
PER = PIECE // HEAD_DIM
HALO = 16
STRIP = 64
LAG = 2
F32 = jnp.float32
BF16 = jnp.bfloat16
MESH = pl.DeviceIdType.MESH


def dot(a, b):
    return jnp.dot(a, b, preferred_element_type=F32)


def silu(x):
    y = 0.5 * x
    return y + y * jnp.tanh(y)


def kernel(
    n,
    x_hbm, gate_hbm, tapf, tapr, step_ref, decay, skip, y_hbm, scale_ref,
    xpad, gate_v, vcat, accw, stf, str_, cinf, cinr, sbf, sbr,
    colc, cfs, ces, rowc, aft, sel, drow, gf_ref, gr_ref, kq, kt, ssq, y_v, xf0, xf1,
    local_sem, halo_send, halo_recv, sendf, recvf, sendr, recvr, out_sem,
):
    me = lax.axis_index("seq")
    has_left = me > 0
    has_right = me < n - 1
    left = lax.rem(me + n - 1, n)
    right = lax.rem(me + 1, n)

    load_x = pltpu.make_async_copy(x_hbm, xpad.at[pl.ds(HALO, BLOCK)], local_sem.at[0])
    load_gate = pltpu.make_async_copy(gate_hbm, gate_v, local_sem.at[1])
    load_x.start()
    load_gate.start()

    barrier = pltpu.get_barrier_semaphore()

    @pl.when(has_left)
    def _():
        pl.semaphore_signal(barrier, inc=1, device_id={"seq": left}, device_id_type=MESH)

    @pl.when(has_right)
    def _():
        pl.semaphore_signal(barrier, inc=1, device_id={"seq": right}, device_id_type=MESH)

    pl.semaphore_wait(barrier, has_left.astype(jnp.int32) + has_right.astype(jnp.int32))

    to_right = pltpu.make_async_remote_copy(
        src_ref=x_hbm.at[pl.ds(BLOCK - HALO, HALO)],
        dst_ref=xpad.at[pl.ds(0, HALO)],
        send_sem=halo_send.at[0],
        recv_sem=halo_recv.at[0],
        device_id={"seq": right},
        device_id_type=MESH,
    )
    to_left = pltpu.make_async_remote_copy(
        src_ref=x_hbm.at[pl.ds(0, HALO)],
        dst_ref=xpad.at[pl.ds(HALO + BLOCK, HALO)],
        send_sem=halo_send.at[1],
        recv_sem=halo_recv.at[1],
        device_id={"seq": left},
        device_id_type=MESH,
    )

    @pl.when(has_right)
    def _():
        to_right.start()

    @pl.when(has_left)
    def _():
        to_left.start()

    @pl.when(jnp.logical_not(has_left))
    def _():
        cinf[...] = jnp.zeros(cinf.shape, BF16)
        xpad[0:HALO, :] = jnp.zeros((HALO, xpad.shape[1]), BF16)

    @pl.when(jnp.logical_not(has_right))
    def _():
        cinr[...] = jnp.zeros(cinr.shape, BF16)
        xpad[HALO + BLOCK :, :] = jnp.zeros((HALO, xpad.shape[1]), BF16)

    for h in range(HEADS):
        ces[h : h + 1, :] = step_ref[h : h + 1, :] * (-decay[h])
    logs = ces[...]
    row_i = lax.broadcasted_iota(jnp.int32, (BLOCK, BLOCK), 0)
    col_i = lax.broadcasted_iota(jnp.int32, (BLOCK, BLOCK), 1)
    upto = jnp.where(row_i <= col_i, 1.0, 0.0).astype(F32)
    cum = jnp.dot(logs, upto, preferred_element_type=F32, precision=lax.Precision.HIGHEST)
    before = cum - logs
    total = cum[:, BLOCK - 1 : BLOCK]
    steps = step_ref[...]
    log_steps = jnp.log(steps)
    cfs[...] = cum - log_steps
    ces[...] = before + log_steps
    for p in range(PIECES):
        rowc[p, 0:PER, :] = cfs[p * PER : (p + 1) * PER, :]
        rowc[p, PER : 2 * PER, :] = ces[p * PER : (p + 1) * PER, :]
    columns = jnp.transpose(jnp.concatenate([cum, before], axis=0))
    for p in range(PIECES):
        shift = (STATE - PER * p) % STATE
        colc[p] = pltpu.roll(columns, shift, axis=1) if shift else columns
    factors = (
        steps * jnp.exp(total - cum),
        steps * jnp.exp(before),
        jnp.exp(cum),
        jnp.exp(total - before),
    )
    parts = []
    for f in factors:
        high = f.astype(BF16).astype(F32)
        parts.append((high, f - high))
    for v in range(PIECES // 4):
        rows = []
        for u in (2 * v, 2 * v + 1):
            for high, low in parts:
                rows.append(high[8 * u : 8 * u + 8])
                rows.append(low[8 * u : 8 * u + 8])
        aft[v] = jnp.transpose(jnp.concatenate(rows, axis=0)).astype(BF16)
    sel_row = lax.broadcasted_iota(jnp.int32, (STATE, PIECE), 0)
    sel_col = lax.broadcasted_iota(jnp.int32, (STATE, PIECE), 1) >> 6
    base = sel_row - sel_col
    for q in range(4):
        for f in range(4):
            off = (q // 2) * 64 + f * 16 + (q % 2) * 4
            hit = jnp.logical_or(base == off, base == off + 8)
            sel[q, :, f * PIECE : (f + 1) * PIECE] = jnp.where(hit, 1.0, 0.0).astype(BF16)

    half = BLOCK // 2
    xfs = (xf0, xf1)
    load_x.wait()

    @pl.when(has_right)
    def _():
        to_right.wait_send()
        to_left.wait_recv()

    @pl.when(has_left)
    def _():
        to_right.wait_recv()
        to_left.wait_send()

    def conv(cols, xf):
        xf[...] = xpad[:, cols].astype(F32)
        fw = tapf[:, cols]
        rv = tapr[:, cols]
        for r in range(0, BLOCK, STRIP):
            ahead = behind = None
            for k in range(WIDTH):
                a = fw[k : k + 1] * xf[pl.ds(HALO + r + k - (WIDTH - 1), STRIP), :]
                b = rv[k : k + 1] * xf[pl.ds(HALO + r + WIDTH - 1 - k, STRIP), :]
                ahead = a if ahead is None else ahead + a
                behind = b if behind is None else behind + b
            yield r, silu(ahead).astype(BF16), silu(behind).astype(BF16)

    for which in range(2):
        for r, a, b in conv(pl.ds(INNER + which * STATE, STATE), xfs[which]):
            kq[which, r : r + STRIP, :] = a
            kq[2 + which, r : r + STRIP, :] = b
    lo, hi = slice(0, half), slice(half, BLOCK)
    for i in range(2):
        keys = jnp.transpose(kq[2 * i].astype(F32)).astype(BF16)
        kt[i, :, lo] = keys[:, hi]
        kt[i, :, hi] = keys[:, lo]
        inside = row_i >= col_i if i == 0 else row_i <= col_i
        (gf_ref, gr_ref)[i][...] = jnp.where(inside, dot(kq[2 * i + 1], keys), 0.0).astype(BF16)
    load_gate.wait()

    lane = lax.broadcasted_iota(jnp.int32, (1, STATE), 1)
    first_half = lane < HEAD_DIM

    def convolve(p):
        for c in range(PIECE // STATE):
            cols = pl.ds(pl.multiple_of(p * PIECE + c * STATE, STATE), STATE)
            for r, a, b in conv(cols, xfs[c]):
                at = (r + half) % BLOCK
                vcat[p, pl.ds(at, STRIP), pl.ds(c * STATE, STATE)] = a
                vcat[p, pl.ds(BLOCK + at, STRIP), pl.ds(c * STATE, STATE)] = b

    def states(p):
        v = p // 4
        q = lax.rem(p, 4)
        ends = dot(aft[v, BLOCK - 16 : BLOCK, :], sel[q, :, 2 * PIECE : 3 * PIECE])
        drow[p, 0:1, :] = ends[15:16, :]
        for i, st in enumerate((stf, str_)):
            wide = dot(aft[v], sel[q, :, i * PIECE : (i + 1) * PIECE])
            top = i * BLOCK
            w = jnp.concatenate(
                [
                    (vcat[p, top : top + half, :].astype(F32) * wide[hi]).astype(BF16),
                    (vcat[p, top + half : top + BLOCK, :].astype(F32) * wide[lo]).astype(BF16),
                ],
                axis=0,
            )
            st[p] = dot(kt[i], w)

    def hop(p, forward):
        sb, cin = (sbf, cinf) if forward else (sbr, cinr)
        send, recv = (sendf, recvf) if forward else (sendr, recvr)
        return pltpu.make_async_remote_copy(
            src_ref=sb.at[p],
            dst_ref=cin.at[p],
            send_sem=send.at[p],
            recv_sem=recv.at[p],
            device_id={"seq": right if forward else left},
            device_id_type=MESH,
        )

    def relay(p, forward):
        copy = hop(p, forward)
        cin, sb, st = (cinf, sbf, stf) if forward else (cinr, sbr, str_)
        takes, gives = (has_left, has_right) if forward else (has_right, has_left)

        @pl.when(takes)
        def _():
            copy.wait_recv()

        @pl.when(gives)
        def _():
            sb[p] = (st[p] + drow[p, 0:1, :] * cin[p].astype(F32)).astype(BF16)
            copy.start()

    def within(p):
        for pair in range(PER // 2):
            lanes = slice(pair * STATE, (pair + 1) * STATE)
            tops, lows = [], []
            for j in (2 * pair, 2 * pair + 1):
                cft = jnp.broadcast_to(colc[p, :, j : j + 1], (BLOCK, half))
                cet = jnp.broadcast_to(colc[p, :, 64 + j : 65 + j], (BLOCK, half))
                ra = rowc[p, j : j + 1, :]
                rb = rowc[p, PER + j : PER + j + 1, :]
                d00 = jnp.exp(jnp.minimum(cft[lo] - ra[:, lo], rb[:, lo] - cet[lo])).astype(BF16)
                d01 = jnp.exp(rb[:, hi] - cet[lo]).astype(BF16)
                tops.append(
                    jnp.concatenate(
                        [gf_ref[lo, lo] * d00, gr_ref[lo, hi] * d01, gr_ref[lo, lo] * d00], axis=1
                    )
                )
                d11 = jnp.exp(jnp.minimum(cft[hi] - ra[:, hi], rb[:, hi] - cet[hi])).astype(BF16)
                d10 = jnp.exp(cft[hi] - ra[:, lo]).astype(BF16)
                lows.append(
                    jnp.concatenate(
                        [gf_ref[hi, hi] * d11, gf_ref[hi, lo] * d10, gr_ref[hi, hi] * d11], axis=1
                    )
                )
            top = dot(jnp.concatenate(tops, axis=0), vcat[p, half : 2 * BLOCK, lanes])
            low = dot(jnp.concatenate(lows, axis=0), vcat[p, 0 : BLOCK + half, lanes])
            skip_row = jnp.where(first_half, skip[p * PER + 2 * pair], skip[p * PER + 2 * pair + 1])
            for rows, res, at in ((lo, top, half), (hi, low, 0)):
                direct = skip_row * vcat[p, at : at + half, lanes].astype(F32)
                accw[p, rows, lanes] = direct + jnp.where(first_half, res[:half], res[half:])

    def y_copy(p):
        cols = pl.ds(pl.multiple_of(p * PIECE, PIECE), PIECE)
        return pltpu.make_async_copy(y_v.at[p], y_hbm.at[:, cols], out_sem.at[p])

    def finish(p):
        v = p // 4
        q = lax.rem(p, 4)
        cols = pl.ds(pl.multiple_of(p * PIECE, PIECE), PIECE)
        growf = dot(aft[v], sel[q, :, 2 * PIECE : 3 * PIECE])
        growr = dot(aft[v], sel[q, :, 3 * PIECE : 4 * PIECE])
        f = dot(kq[1], cinf[p])
        r = dot(kq[3], cinr[p])
        gate = silu(gate_v[:, cols].astype(F32))
        y = (accw[p] + (growf * f + growr * r)) * gate
        y_v[p] = y.astype(BF16)
        y = y * y
        ssq[...] = ssq[...] + (y[:, :STATE] + y[:, STATE:])
        y_copy(p).start()

    ssq[...] = jnp.zeros_like(ssq)
    second = 1 + max(PIECES, LAG * (n - 1))

    def relays(k):
        for forward, late in ((True, 1 + LAG * me), (False, 1 + LAG * (n - 1 - me))):
            p = k - late

            @pl.when(jnp.logical_and(p >= 0, p < PIECES))
            def _():
                relay(p, forward)

    convolve(0)

    def slot_a(k, carry):
        states(k - 1)
        convolve(k)
        relays(k)
        return carry

    lax.fori_loop(1, PIECES, slot_a, 0)
    states(PIECES - 1)

    def slot_idle(k, carry):
        relays(k)
        return carry

    lax.fori_loop(PIECES, second, slot_idle, 0)
    relays(second)
    within(0)

    def slot_b(k, carry):
        relays(k)
        finish(k - second - 1)
        within(k - second)
        return carry

    lax.fori_loop(second + 1, second + PIECES, slot_b, 0)
    finish(PIECES - 1)
    mean = jnp.sum(ssq[...], axis=1, keepdims=True) * (1.0 / INNER)
    scale_ref[...] = jnp.broadcast_to(lax.rsqrt(mean + 1e-05), scale_ref.shape)

    @pl.when(has_right)
    def _():
        def done(p, carry):
            hop(p, True).wait_send()
            return carry

        lax.fori_loop(0, PIECES, done, 0)

    @pl.when(has_left)
    def _():
        def done(p, carry):
            hop(p, False).wait_send()
            return carry

        lax.fori_loop(0, PIECES, done, 0)

    def stored(p, carry):
        y_copy(p).wait()
        return carry

    lax.fori_loop(0, PIECES, stored, 0)


def scale_rows(y_hbm, scale_ref, gain_ref, out_hbm, y_v, out_v, in_sem, out_sem):
    parts = [pl.ds(r, STRIP) for r in range(0, BLOCK, STRIP)]
    loads = [pltpu.make_async_copy(y_hbm.at[s], y_v.at[s], in_sem.at[i]) for i, s in enumerate(parts)]
    stores = [
        pltpu.make_async_copy(out_v.at[s], out_hbm.at[s], out_sem.at[i]) for i, s in enumerate(parts)
    ]
    for load in loads:
        load.start()
    for i, rows in enumerate(parts):
        loads[i].wait()
        scale = scale_ref[rows, :]
        for c in range(0, INNER, STATE):
            cols = pl.ds(c, STATE)
            out_v[rows, cols] = (y_v[rows, cols].astype(F32) * scale * gain_ref[:, cols]).astype(BF16)
        stores[i].start()
    for store in stores:
        store.wait()


def per_device(
    mixer_input, gate_input, conv_forward, conv_reverse, step_size, decay_rate, skip_scale, norm_gain
):
    n = lax.axis_size("seq")
    vmem = pl.BlockSpec(memory_space=pltpu.VMEM)
    smem = pl.BlockSpec(memory_space=pltpu.SMEM)
    hbm = pl.BlockSpec(memory_space=pl.ANY)
    piece = (PIECES, BLOCK, PIECE)
    state = (PIECES, STATE, PIECE)
    dma = pltpu.SemaphoreType.DMA
    y, scale = pl.pallas_call(
        functools.partial(kernel, n),
        out_shape=(
            jax.ShapeDtypeStruct((BLOCK, INNER), BF16),
            jax.ShapeDtypeStruct((BLOCK, STATE), F32),
        ),
        in_specs=[hbm, hbm, vmem, vmem, vmem, smem, smem],
        out_specs=(hbm, vmem),
        scratch_shapes=[
            pltpu.VMEM((BLOCK + 2 * HALO, INNER + 2 * STATE), BF16),
            pltpu.VMEM((BLOCK, INNER), BF16),
            pltpu.VMEM((PIECES, 2 * BLOCK, PIECE), BF16),
            pltpu.VMEM(piece, F32),
            pltpu.VMEM(state, F32),
            pltpu.VMEM(state, F32),
            pltpu.VMEM(state, BF16),
            pltpu.VMEM(state, BF16),
            pltpu.VMEM(state, BF16),
            pltpu.VMEM(state, BF16),
            pltpu.VMEM((PIECES, BLOCK, STATE), F32),
            pltpu.VMEM((HEADS, BLOCK), F32),
            pltpu.VMEM((HEADS, BLOCK), F32),
            pltpu.VMEM((PIECES, 2 * PER, BLOCK), F32),
            pltpu.VMEM((PIECES // 4, BLOCK, STATE), BF16),
            pltpu.VMEM((4, STATE, 4 * PIECE), BF16),
            pltpu.VMEM((PIECES, 8, PIECE), F32),
            pltpu.VMEM((BLOCK, BLOCK), BF16),
            pltpu.VMEM((BLOCK, BLOCK), BF16),
            pltpu.VMEM((4, BLOCK, STATE), BF16),
            pltpu.VMEM((2, STATE, BLOCK), BF16),
            pltpu.VMEM((BLOCK, STATE), F32),
            pltpu.VMEM(piece, BF16),
            pltpu.VMEM((BLOCK + 2 * HALO, STATE), F32),
            pltpu.VMEM((BLOCK + 2 * HALO, STATE), F32),
            dma((2,)),
            dma((2,)),
            dma((2,)),
            dma((PIECES,)),
            dma((PIECES,)),
            dma((PIECES,)),
            dma((PIECES,)),
            dma((PIECES,)),
        ],
        compiler_params=pltpu.CompilerParams(
            collective_id=0, has_side_effects=True, vmem_limit_bytes=56 * 1024 * 1024
        ),
        cost_estimate=pl.CostEstimate(flops=3 * 10**9, bytes_accessed=7 * 10**6, transcendentals=10**7),
        name="mixer",
    )(
        mixer_input, gate_input, conv_forward, conv_reverse, step_size, decay_rate, skip_scale
    )
    dma = pltpu.SemaphoreType.DMA
    parts = BLOCK // STRIP
    return pl.pallas_call(
        scale_rows,
        out_shape=jax.ShapeDtypeStruct((BLOCK, INNER), BF16),
        in_specs=[hbm, vmem, vmem],
        out_specs=hbm,
        scratch_shapes=[
            pltpu.VMEM((BLOCK, INNER), BF16),
            pltpu.VMEM((BLOCK, INNER), BF16),
            dma((parts,)),
            dma((parts,)),
        ],
        compiler_params=pltpu.CompilerParams(vmem_limit_bytes=60 * 1024 * 1024),
        cost_estimate=pl.CostEstimate(flops=2 * 10**6, bytes_accessed=4 * 10**6, transcendentals=0),
        name="scale_rows",
    )(y, scale, norm_gain.reshape(1, INNER))


def solution(mesh):
    in_specs = (
        P(("row", "seq"), None),
        P(("row", "seq"), None),
        P(),
        P(),
        P(None, ("row", "seq")),
        P("row"),
        P(),
        P(),
    )
    out_specs = P(("row", "seq"), None)
    return jax.shard_map(
        per_device, mesh=mesh, in_specs=in_specs, out_specs=out_specs, check_vma=False
    )
```

```python
import functools

import jax
import jax.numpy as jnp
from jax import lax
from jax.experimental import pallas as pl
from jax.experimental.pallas import tpu as pltpu
from jax.sharding import PartitionSpec as P

HEADS = 64
HEAD_DIM = 64
STATE = 128
WIDTH = 4
BLOCK = 256
INNER = HEADS * HEAD_DIM
PIECE = 256
PIECES = INNER // PIECE
PER = PIECE // HEAD_DIM
HALO = 16
STRIP = 64
LAG = 4
F32 = jnp.float32
BF16 = jnp.bfloat16
MESH = pl.DeviceIdType.MESH


def dot(a, b):
    return jnp.dot(a, b, preferred_element_type=F32)


def silu(x):
    y = 0.5 * x
    return y + y * jnp.tanh(y)


def kernel(
    n,
    x_hbm, gate_hbm, tapf, tapr, step_ref, decay, skip, y_hbm, scale_ref,
    xpad, gate_v, vcat, accw, stf, str_, cinf, cinr, sbf, sbr,
    colc, cfs, ces, rowc, aft, sel, drow, gf_ref, gr_ref, kq, kt, ssq, y_v, xf0, xf1,
    local_sem, halo_send, halo_recv, sendf, recvf, sendr, recvr, out_sem,
):
    me = lax.axis_index("seq")
    has_left = me > 0
    has_right = me < n - 1
    left = lax.rem(me + n - 1, n)
    right = lax.rem(me + 1, n)

    load_x = pltpu.make_async_copy(x_hbm, xpad.at[pl.ds(HALO, BLOCK)], local_sem.at[0])
    load_gate = pltpu.make_async_copy(gate_hbm, gate_v, local_sem.at[1])
    load_x.start()
    load_gate.start()

    barrier = pltpu.get_barrier_semaphore()

    @pl.when(has_left)
    def _():
        pl.semaphore_signal(barrier, inc=1, device_id={"seq": left}, device_id_type=MESH)

    @pl.when(has_right)
    def _():
        pl.semaphore_signal(barrier, inc=1, device_id={"seq": right}, device_id_type=MESH)

    pl.semaphore_wait(barrier, has_left.astype(jnp.int32) + has_right.astype(jnp.int32))

    to_right = pltpu.make_async_remote_copy(
        src_ref=x_hbm.at[pl.ds(BLOCK - HALO, HALO)],
        dst_ref=xpad.at[pl.ds(0, HALO)],
        send_sem=halo_send.at[0],
        recv_sem=halo_recv.at[0],
        device_id={"seq": right},
        device_id_type=MESH,
    )
    to_left = pltpu.make_async_remote_copy(
        src_ref=x_hbm.at[pl.ds(0, HALO)],
        dst_ref=xpad.at[pl.ds(HALO + BLOCK, HALO)],
        send_sem=halo_send.at[1],
        recv_sem=halo_recv.at[1],
        device_id={"seq": left},
        device_id_type=MESH,
    )

    @pl.when(has_right)
    def _():
        to_right.start()

    @pl.when(has_left)
    def _():
        to_left.start()

    @pl.when(jnp.logical_not(has_left))
    def _():
        cinf[...] = jnp.zeros(cinf.shape, BF16)
        xpad[0:HALO, :] = jnp.zeros((HALO, xpad.shape[1]), BF16)

    @pl.when(jnp.logical_not(has_right))
    def _():
        cinr[...] = jnp.zeros(cinr.shape, BF16)
        xpad[HALO + BLOCK :, :] = jnp.zeros((HALO, xpad.shape[1]), BF16)

    for h in range(HEADS):
        ces[h : h + 1, :] = step_ref[h : h + 1, :] * (-decay[h])
    logs = ces[...]
    row_i = lax.broadcasted_iota(jnp.int32, (BLOCK, BLOCK), 0)
    col_i = lax.broadcasted_iota(jnp.int32, (BLOCK, BLOCK), 1)
    upto = jnp.where(row_i <= col_i, 1.0, 0.0).astype(F32)
    cum = jnp.dot(logs, upto, preferred_element_type=F32, precision=lax.Precision.HIGHEST)
    before = cum - logs
    total = cum[:, BLOCK - 1 : BLOCK]
    steps = step_ref[...]
    log_steps = jnp.log(steps)
    cfs[...] = cum - log_steps
    ces[...] = before + log_steps
    for p in range(PIECES):
        rowc[p, 0:PER, :] = cfs[p * PER : (p + 1) * PER, :]
        rowc[p, PER : 2 * PER, :] = ces[p * PER : (p + 1) * PER, :]
    columns = jnp.transpose(jnp.concatenate([cum, before], axis=0))
    for p in range(PIECES):
        shift = (STATE - PER * p) % STATE
        colc[p] = pltpu.roll(columns, shift, axis=1) if shift else columns
    factors = (
        steps * jnp.exp(total - cum),
        steps * jnp.exp(before),
        jnp.exp(cum),
        jnp.exp(total - before),
    )
    parts = []
    for f in factors:
        high = f.astype(BF16).astype(F32)
        parts.append((high, f - high))
    for v in range(PIECES // 4):
        rows = []
        for u in (2 * v, 2 * v + 1):
            for high, low in parts:
                rows.append(high[8 * u : 8 * u + 8])
                rows.append(low[8 * u : 8 * u + 8])
        aft[v] = jnp.transpose(jnp.concatenate(rows, axis=0)).astype(BF16)
    sel_row = lax.broadcasted_iota(jnp.int32, (STATE, PIECE), 0)
    sel_col = lax.broadcasted_iota(jnp.int32, (STATE, PIECE), 1) >> 6
    base = sel_row - sel_col
    for q in range(4):
        for f in range(4):
            off = (q // 2) * 64 + f * 16 + (q % 2) * 4
            hit = jnp.logical_or(base == off, base == off + 8)
            sel[q, :, f * PIECE : (f + 1) * PIECE] = jnp.where(hit, 1.0, 0.0).astype(BF16)

    half = BLOCK // 2
    xfs = (xf0, xf1)
    load_x.wait()

    @pl.when(has_right)
    def _():
        to_right.wait_send()
        to_left.wait_recv()

    @pl.when(has_left)
    def _():
        to_right.wait_recv()
        to_left.wait_send()

    def conv(cols, xf):
        xf[...] = xpad[:, cols].astype(F32)
        fw = tapf[:, cols]
        rv = tapr[:, cols]
        for r in range(0, BLOCK, STRIP):
            ahead = behind = None
            for k in range(WIDTH):
                a = fw[k : k + 1] * xf[pl.ds(HALO + r + k - (WIDTH - 1), STRIP), :]
                b = rv[k : k + 1] * xf[pl.ds(HALO + r + WIDTH - 1 - k, STRIP), :]
                ahead = a if ahead is None else ahead + a
                behind = b if behind is None else behind + b
            yield r, silu(ahead).astype(BF16), silu(behind).astype(BF16)

    for which in range(2):
        for r, a, b in conv(pl.ds(INNER + which * STATE, STATE), xfs[which]):
            kq[which, r : r + STRIP, :] = a
            kq[2 + which, r : r + STRIP, :] = b
    lo, hi = slice(0, half), slice(half, BLOCK)
    for i in range(2):
        keys = jnp.transpose(kq[2 * i].astype(F32)).astype(BF16)
        kt[i, :, lo] = keys[:, hi]
        kt[i, :, hi] = keys[:, lo]
        inside = row_i >= col_i if i == 0 else row_i <= col_i
        (gf_ref, gr_ref)[i][...] = jnp.where(inside, dot(kq[2 * i + 1], keys), 0.0).astype(BF16)
    load_gate.wait()

    lane = lax.broadcasted_iota(jnp.int32, (1, STATE), 1)
    first_half = lane < HEAD_DIM

    def convolve(p):
        for c in range(PIECE // STATE):
            cols = pl.ds(pl.multiple_of(p * PIECE + c * STATE, STATE), STATE)
            for r, a, b in conv(cols, xfs[c]):
                at = (r + half) % BLOCK
                vcat[p, pl.ds(at, STRIP), pl.ds(c * STATE, STATE)] = a
                vcat[p, pl.ds(BLOCK + at, STRIP), pl.ds(c * STATE, STATE)] = b

    def states(p):
        v = p // 4
        q = lax.rem(p, 4)
        ends = dot(aft[v, BLOCK - 16 : BLOCK, :], sel[q, :, 2 * PIECE : 3 * PIECE])
        drow[p, 0:1, :] = ends[15:16, :]
        for i, st in enumerate((stf, str_)):
            wide = dot(aft[v], sel[q, :, i * PIECE : (i + 1) * PIECE])
            top = i * BLOCK
            w = jnp.concatenate(
                [
                    (vcat[p, top : top + half, :].astype(F32) * wide[hi]).astype(BF16),
                    (vcat[p, top + half : top + BLOCK, :].astype(F32) * wide[lo]).astype(BF16),
                ],
                axis=0,
            )
            st[p] = dot(kt[i], w)

    def hop(p, forward):
        sb, cin = (sbf, cinf) if forward else (sbr, cinr)
        send, recv = (sendf, recvf) if forward else (sendr, recvr)
        return pltpu.make_async_remote_copy(
            src_ref=sb.at[p],
            dst_ref=cin.at[p],
            send_sem=send.at[p],
            recv_sem=recv.at[p],
            device_id={"seq": right if forward else left},
            device_id_type=MESH,
        )

    def relay(p, forward):
        copy = hop(p, forward)
        cin, sb, st = (cinf, sbf, stf) if forward else (cinr, sbr, str_)
        takes, gives = (has_left, has_right) if forward else (has_right, has_left)

        @pl.when(takes)
        def _():
            copy.wait_recv()

        @pl.when(gives)
        def _():
            sb[p] = (st[p] + drow[p, 0:1, :] * cin[p].astype(F32)).astype(BF16)
            copy.start()

    def within(p):
        for pair in range(PER // 2):
            lanes = slice(pair * STATE, (pair + 1) * STATE)
            tops, lows = [], []
            for j in (2 * pair, 2 * pair + 1):
                cft = jnp.broadcast_to(colc[p, :, j : j + 1], (BLOCK, half))
                cet = jnp.broadcast_to(colc[p, :, 64 + j : 65 + j], (BLOCK, half))
                ra = rowc[p, j : j + 1, :]
                rb = rowc[p, PER + j : PER + j + 1, :]
                d00 = jnp.exp(jnp.minimum(cft[lo] - ra[:, lo], rb[:, lo] - cet[lo])).astype(BF16)
                d01 = jnp.exp(rb[:, hi] - cet[lo]).astype(BF16)
                tops.append(
                    jnp.concatenate(
                        [gf_ref[lo, lo] * d00, gr_ref[lo, hi] * d01, gr_ref[lo, lo] * d00], axis=1
                    )
                )
                d11 = jnp.exp(jnp.minimum(cft[hi] - ra[:, hi], rb[:, hi] - cet[hi])).astype(BF16)
                d10 = jnp.exp(cft[hi] - ra[:, lo]).astype(BF16)
                lows.append(
                    jnp.concatenate(
                        [gf_ref[hi, hi] * d11, gf_ref[hi, lo] * d10, gr_ref[hi, hi] * d11], axis=1
                    )
                )
            top = dot(jnp.concatenate(tops, axis=0), vcat[p, half : 2 * BLOCK, lanes])
            low = dot(jnp.concatenate(lows, axis=0), vcat[p, 0 : BLOCK + half, lanes])
            skip_row = jnp.where(first_half, skip[p * PER + 2 * pair], skip[p * PER + 2 * pair + 1])
            for rows, res, at in ((lo, top, half), (hi, low, 0)):
                direct = skip_row * vcat[p, at : at + half, lanes].astype(F32)
                accw[p, rows, lanes] = direct + jnp.where(first_half, res[:half], res[half:])

    def y_copy(p):
        cols = pl.ds(pl.multiple_of(p * PIECE, PIECE), PIECE)
        return pltpu.make_async_copy(y_v.at[p], y_hbm.at[:, cols], out_sem.at[p])

    def finish(p):
        v = p // 4
        q = lax.rem(p, 4)
        cols = pl.ds(pl.multiple_of(p * PIECE, PIECE), PIECE)
        growf = dot(aft[v], sel[q, :, 2 * PIECE : 3 * PIECE])
        growr = dot(aft[v], sel[q, :, 3 * PIECE : 4 * PIECE])
        f = dot(kq[1], cinf[p])
        r = dot(kq[3], cinr[p])
        gate = silu(gate_v[:, cols].astype(F32))
        y = (accw[p] + (growf * f + growr * r)) * gate
        y_v[p] = y.astype(BF16)
        y = y * y
        ssq[...] = ssq[...] + (y[:, :STATE] + y[:, STATE:])
        y_copy(p).start()

    ssq[...] = jnp.zeros_like(ssq)
    ready = jnp.maximum(PIECES + 1, 1 + LAG * jnp.maximum(me, n - 1 - me))

    def relays(k):
        for forward, late in ((True, 1 + LAG * me), (False, 1 + LAG * (n - 1 - me))):
            p = k - late

            @pl.when(jnp.logical_and(p >= 0, p < PIECES))
            def _():
                relay(p, forward)

    convolve(0)

    def slot_a(k, carry):
        states(k - 1)
        convolve(k)
        relays(k)
        return carry

    lax.fori_loop(1, PIECES, slot_a, 0)
    states(PIECES - 1)

    def slot_b(k, carry):
        relays(k)

        @pl.when(k >= ready)
        def _():
            finish(k - ready)
            within(k - PIECES)

        @pl.when(k < ready)
        def _():
            within(k - PIECES)

        return carry

    lax.fori_loop(PIECES, 2 * PIECES, slot_b, 0)

    def slot_c(k, carry):
        relays(k)

        @pl.when(k >= ready)
        def _():
            finish(k - ready)

        return carry

    lax.fori_loop(2 * PIECES, ready + PIECES, slot_c, 0)
    mean = jnp.sum(ssq[...], axis=1, keepdims=True) * (1.0 / INNER)
    scale_ref[...] = jnp.broadcast_to(lax.rsqrt(mean + 1e-05), scale_ref.shape)

    @pl.when(has_right)
    def _():
        def done(p, carry):
            hop(p, True).wait_send()
            return carry

        lax.fori_loop(0, PIECES, done, 0)

    @pl.when(has_left)
    def _():
        def done(p, carry):
            hop(p, False).wait_send()
            return carry

        lax.fori_loop(0, PIECES, done, 0)

    def stored(p, carry):
        y_copy(p).wait()
        return carry

    lax.fori_loop(0, PIECES, stored, 0)


def scale_rows(y_hbm, scale_ref, gain_ref, out_hbm, y_v, out_v, in_sem, out_sem):
    parts = [pl.ds(r, STRIP) for r in range(0, BLOCK, STRIP)]
    loads = [pltpu.make_async_copy(y_hbm.at[s], y_v.at[s], in_sem.at[i]) for i, s in enumerate(parts)]
    stores = [
        pltpu.make_async_copy(out_v.at[s], out_hbm.at[s], out_sem.at[i]) for i, s in enumerate(parts)
    ]
    for load in loads:
        load.start()
    for i, rows in enumerate(parts):
        loads[i].wait()
        scale = scale_ref[rows, :]
        for c in range(0, INNER, STATE):
            cols = pl.ds(c, STATE)
            out_v[rows, cols] = (y_v[rows, cols].astype(F32) * scale * gain_ref[:, cols]).astype(BF16)
        stores[i].start()
    for store in stores:
        store.wait()


def per_device(
    mixer_input, gate_input, conv_forward, conv_reverse, step_size, decay_rate, skip_scale, norm_gain
):
    n = lax.axis_size("seq")
    vmem = pl.BlockSpec(memory_space=pltpu.VMEM)
    smem = pl.BlockSpec(memory_space=pltpu.SMEM)
    hbm = pl.BlockSpec(memory_space=pl.ANY)
    piece = (PIECES, BLOCK, PIECE)
    state = (PIECES, STATE, PIECE)
    dma = pltpu.SemaphoreType.DMA
    y, scale = pl.pallas_call(
        functools.partial(kernel, n),
        out_shape=(
            jax.ShapeDtypeStruct((BLOCK, INNER), BF16),
            jax.ShapeDtypeStruct((BLOCK, STATE), F32),
        ),
        in_specs=[hbm, hbm, vmem, vmem, vmem, smem, smem],
        out_specs=(hbm, vmem),
        scratch_shapes=[
            pltpu.VMEM((BLOCK + 2 * HALO, INNER + 2 * STATE), BF16),
            pltpu.VMEM((BLOCK, INNER), BF16),
            pltpu.VMEM((PIECES, 2 * BLOCK, PIECE), BF16),
            pltpu.VMEM(piece, F32),
            pltpu.VMEM(state, F32),
            pltpu.VMEM(state, F32),
            pltpu.VMEM(state, BF16),
            pltpu.VMEM(state, BF16),
            pltpu.VMEM(state, BF16),
            pltpu.VMEM(state, BF16),
            pltpu.VMEM((PIECES, BLOCK, STATE), F32),
            pltpu.VMEM((HEADS, BLOCK), F32),
            pltpu.VMEM((HEADS, BLOCK), F32),
            pltpu.VMEM((PIECES, 2 * PER, BLOCK), F32),
            pltpu.VMEM((PIECES // 4, BLOCK, STATE), BF16),
            pltpu.VMEM((4, STATE, 4 * PIECE), BF16),
            pltpu.VMEM((PIECES, 8, PIECE), F32),
            pltpu.VMEM((BLOCK, BLOCK), BF16),
            pltpu.VMEM((BLOCK, BLOCK), BF16),
            pltpu.VMEM((4, BLOCK, STATE), BF16),
            pltpu.VMEM((2, STATE, BLOCK), BF16),
            pltpu.VMEM((BLOCK, STATE), F32),
            pltpu.VMEM(piece, BF16),
            pltpu.VMEM((BLOCK + 2 * HALO, STATE), F32),
            pltpu.VMEM((BLOCK + 2 * HALO, STATE), F32),
            dma((2,)),
            dma((2,)),
            dma((2,)),
            dma((PIECES,)),
            dma((PIECES,)),
            dma((PIECES,)),
            dma((PIECES,)),
            dma((PIECES,)),
        ],
        compiler_params=pltpu.CompilerParams(
            collective_id=0, has_side_effects=True, vmem_limit_bytes=56 * 1024 * 1024
        ),
        cost_estimate=pl.CostEstimate(flops=3 * 10**9, bytes_accessed=7 * 10**6, transcendentals=10**7),
        name="mixer",
    )(
        mixer_input, gate_input, conv_forward, conv_reverse, step_size, decay_rate, skip_scale
    )
    dma = pltpu.SemaphoreType.DMA
    parts = BLOCK // STRIP
    return pl.pallas_call(
        scale_rows,
        out_shape=jax.ShapeDtypeStruct((BLOCK, INNER), BF16),
        in_specs=[hbm, vmem, vmem],
        out_specs=hbm,
        scratch_shapes=[
            pltpu.VMEM((BLOCK, INNER), BF16),
            pltpu.VMEM((BLOCK, INNER), BF16),
            dma((parts,)),
            dma((parts,)),
        ],
        compiler_params=pltpu.CompilerParams(vmem_limit_bytes=60 * 1024 * 1024),
        cost_estimate=pl.CostEstimate(flops=2 * 10**6, bytes_accessed=4 * 10**6, transcendentals=0),
        name="scale_rows",
    )(y, scale, norm_gain.reshape(1, INNER))


def solution(mesh):
    in_specs = (
        P(("row", "seq"), None),
        P(("row", "seq"), None),
        P(),
        P(),
        P(None, ("row", "seq")),
        P("row"),
        P(),
        P(),
    )
    out_specs = P(("row", "seq"), None)
    return jax.shard_map(
        per_device, mesh=mesh, in_specs=in_specs, out_specs=out_specs, check_vma=False
    )
```

```python
import functools

import jax
import jax.numpy as jnp
from jax import lax
from jax.experimental import pallas as pl
from jax.experimental.pallas import tpu as pltpu
from jax.sharding import PartitionSpec as P

HEADS = 64
HEAD_DIM = 64
STATE = 128
WIDTH = 4
BLOCK = 256
INNER = HEADS * HEAD_DIM
PIECE = 256
PIECES = INNER // PIECE
PER = PIECE // HEAD_DIM
HALO = 16
STRIP = 64
LAG = 3
F32 = jnp.float32
BF16 = jnp.bfloat16
MESH = pl.DeviceIdType.MESH


def dot(a, b):
    return jnp.dot(a, b, preferred_element_type=F32)


def silu(x):
    y = 0.5 * x
    return y + y * jnp.tanh(y)


def kernel(
    n,
    x_hbm, gate_hbm, tapf, tapr, step_ref, decay, skip, y_hbm, scale_ref,
    xpad, gate_v, vcat, accw, stf, str_, midf, midr, cinf, cinr, sbf, sbr,
    colc, cfs, ces, rowc, aft, sel, drow, gf_ref, gr_ref, kq, kt, ssq, y_v, xf0, xf1,
    local_sem, halo_send, halo_recv, sendf, recvf, sendr, recvr, out_sem,
):
    me = lax.axis_index("seq")
    has_left = me > 0
    has_right = me < n - 1
    left = lax.rem(me + n - 1, n)
    right = lax.rem(me + 1, n)

    load_x = pltpu.make_async_copy(x_hbm, xpad.at[pl.ds(HALO, BLOCK)], local_sem.at[0])
    load_gate = pltpu.make_async_copy(gate_hbm, gate_v, local_sem.at[1])
    load_x.start()
    load_gate.start()

    barrier = pltpu.get_barrier_semaphore()

    @pl.when(has_left)
    def _():
        pl.semaphore_signal(barrier, inc=1, device_id={"seq": left}, device_id_type=MESH)

    @pl.when(has_right)
    def _():
        pl.semaphore_signal(barrier, inc=1, device_id={"seq": right}, device_id_type=MESH)

    pl.semaphore_wait(barrier, has_left.astype(jnp.int32) + has_right.astype(jnp.int32))

    to_right = pltpu.make_async_remote_copy(
        src_ref=x_hbm.at[pl.ds(BLOCK - HALO, HALO)],
        dst_ref=xpad.at[pl.ds(0, HALO)],
        send_sem=halo_send.at[0],
        recv_sem=halo_recv.at[0],
        device_id={"seq": right},
        device_id_type=MESH,
    )
    to_left = pltpu.make_async_remote_copy(
        src_ref=x_hbm.at[pl.ds(0, HALO)],
        dst_ref=xpad.at[pl.ds(HALO + BLOCK, HALO)],
        send_sem=halo_send.at[1],
        recv_sem=halo_recv.at[1],
        device_id={"seq": left},
        device_id_type=MESH,
    )

    @pl.when(has_right)
    def _():
        to_right.start()

    @pl.when(has_left)
    def _():
        to_left.start()

    @pl.when(jnp.logical_not(has_left))
    def _():
        cinf[...] = jnp.zeros(cinf.shape, BF16)
        xpad[0:HALO, :] = jnp.zeros((HALO, xpad.shape[1]), BF16)

    @pl.when(jnp.logical_not(has_right))
    def _():
        cinr[...] = jnp.zeros(cinr.shape, BF16)
        xpad[HALO + BLOCK :, :] = jnp.zeros((HALO, xpad.shape[1]), BF16)

    half = BLOCK // 2
    lo, hi = slice(0, half), slice(half, BLOCK)
    for h in range(HEADS):
        ces[h : h + 1, :] = step_ref[h : h + 1, :] * (-decay[h])
    logs = ces[...]
    row_i = lax.broadcasted_iota(jnp.int32, (BLOCK, BLOCK), 0)
    col_i = lax.broadcasted_iota(jnp.int32, (BLOCK, BLOCK), 1)
    upto = jnp.where(row_i <= col_i, 1.0, 0.0).astype(F32)
    cum = jnp.dot(logs, upto, preferred_element_type=F32, precision=lax.Precision.HIGHEST)
    before = cum - logs
    total = cum[:, BLOCK - 1 : BLOCK]
    steps = step_ref[...]
    log_steps = jnp.log(steps)
    cfs[...] = cum - log_steps
    ces[...] = before + log_steps
    for p in range(PIECES):
        rowc[p, 0:PER, :] = cfs[p * PER : (p + 1) * PER, :]
        rowc[p, PER : 2 * PER, :] = ces[p * PER : (p + 1) * PER, :]
    columns = jnp.transpose(jnp.concatenate([cum, before], axis=0))
    for p in range(PIECES):
        shift = (STATE - PER * p) % STATE
        colc[p] = pltpu.roll(columns, shift, axis=1) if shift else columns
    middle = cum[:, half - 1 : half]
    early = lax.broadcasted_iota(jnp.int32, cum.shape, 1) < half
    start = jnp.where(early, 0.0, middle)
    end = jnp.where(early, middle, total)
    factors = (
        steps * jnp.exp(end - cum),
        steps * jnp.exp(before - start),
        jnp.exp(cum - start),
        jnp.exp(end - before),
    )
    parts = []
    for f in factors:
        high = f.astype(BF16).astype(F32)
        parts.append((high, f - high))
    for v in range(PIECES // 4):
        rows = []
        for u in (2 * v, 2 * v + 1):
            for high, low in parts:
                rows.append(high[8 * u : 8 * u + 8])
                rows.append(low[8 * u : 8 * u + 8])
        aft[v] = jnp.transpose(jnp.concatenate(rows, axis=0)).astype(BF16)
    sel_row = lax.broadcasted_iota(jnp.int32, (STATE, PIECE), 0)
    sel_col = lax.broadcasted_iota(jnp.int32, (STATE, PIECE), 1) >> 6
    base = sel_row - sel_col
    for q in range(4):
        for f in range(4):
            off = (q // 2) * 64 + f * 16 + (q % 2) * 4
            hit = jnp.logical_or(base == off, base == off + 8)
            sel[q, :, f * PIECE : (f + 1) * PIECE] = jnp.where(hit, 1.0, 0.0).astype(BF16)

    xfs = (xf0, xf1)
    load_x.wait()

    @pl.when(has_right)
    def _():
        to_right.wait_send()
        to_left.wait_recv()

    @pl.when(has_left)
    def _():
        to_right.wait_recv()
        to_left.wait_send()

    def conv(cols, xf):
        xf[...] = xpad[:, cols].astype(F32)
        fw = tapf[:, cols]
        rv = tapr[:, cols]
        for r in range(0, BLOCK, STRIP):
            ahead = behind = None
            for k in range(WIDTH):
                a = fw[k : k + 1] * xf[pl.ds(HALO + r + k - (WIDTH - 1), STRIP), :]
                b = rv[k : k + 1] * xf[pl.ds(HALO + r + WIDTH - 1 - k, STRIP), :]
                ahead = a if ahead is None else ahead + a
                behind = b if behind is None else behind + b
            yield r, silu(ahead).astype(BF16), silu(behind).astype(BF16)

    for which in range(2):
        for r, a, b in conv(pl.ds(INNER + which * STATE, STATE), xfs[which]):
            kq[which, r : r + STRIP, :] = a
            kq[2 + which, r : r + STRIP, :] = b
    for i in range(2):
        keys = jnp.transpose(kq[2 * i].astype(F32)).astype(BF16)
        kt[i] = keys
        inside = row_i >= col_i if i == 0 else row_i <= col_i
        (gf_ref, gr_ref)[i][...] = jnp.where(inside, dot(kq[2 * i + 1], keys), 0.0).astype(BF16)
    load_gate.wait()

    lane = lax.broadcasted_iota(jnp.int32, (1, STATE), 1)
    first_half = lane < HEAD_DIM

    def convolve(p):
        for c in range(PIECE // STATE):
            cols = pl.ds(pl.multiple_of(p * PIECE + c * STATE, STATE), STATE)
            for r, a, b in conv(cols, xfs[c]):
                at = r // half * BLOCK + r % half
                vcat[p, pl.ds(at, STRIP), pl.ds(c * STATE, STATE)] = a
                vcat[p, pl.ds(half + at, STRIP), pl.ds(c * STATE, STATE)] = b

    def states(p):
        v = p // 4
        q = lax.rem(p, 4)
        for i in range(2):
            ends = dot(aft[v, i * half + half - 16 : (i + 1) * half, :], sel[q, :, 2 * PIECE : 3 * PIECE])
            drow[p, i : i + 1, :] = ends[15:16, :]
        for i, (st, mid) in enumerate(((stf, midf), (str_, midr))):
            wide = dot(aft[v], sel[q, :, i * PIECE : (i + 1) * PIECE])
            top = i * half
            low = (vcat[p, top : top + half, :].astype(F32) * wide[lo]).astype(BF16)
            high = (vcat[p, BLOCK + top : BLOCK + top + half, :].astype(F32) * wide[hi]).astype(BF16)
            low = dot(kt[i, :, lo], low)
            high = dot(kt[i, :, hi], high)
            first, second = (low, high) if i == 0 else (high, low)
            mid[p] = first
            st[p] = second + drow[p, 1 - i : 2 - i, :] * first

    def hop(p, forward):
        sb, cin = (sbf, cinf) if forward else (sbr, cinr)
        send, recv = (sendf, recvf) if forward else (sendr, recvr)
        return pltpu.make_async_remote_copy(
            src_ref=sb.at[p],
            dst_ref=cin.at[p],
            send_sem=send.at[p],
            recv_sem=recv.at[p],
            device_id={"seq": right if forward else left},
            device_id_type=MESH,
        )

    def relay(p, forward):
        copy = hop(p, forward)
        cin, sb, st = (cinf, sbf, stf) if forward else (cinr, sbr, str_)
        takes, gives = (has_left, has_right) if forward else (has_right, has_left)

        @pl.when(takes)
        def _():
            copy.wait_recv()

        @pl.when(gives)
        def _():
            whole = drow[p, 0:1, :] * drow[p, 1:2, :]
            sb[p] = (st[p] + whole * cin[p].astype(F32)).astype(BF16)
            copy.start()

    def within(p):
        for pair in range(PER // 2):
            lanes = slice(pair * STATE, (pair + 1) * STATE)
            tops, lows = [], []
            for j in (2 * pair, 2 * pair + 1):
                cft = jnp.broadcast_to(colc[p, :, j : j + 1], (BLOCK, half))
                cet = jnp.broadcast_to(colc[p, :, 64 + j : 65 + j], (BLOCK, half))
                ra = rowc[p, j : j + 1, :]
                rb = rowc[p, PER + j : PER + j + 1, :]
                for part, rows in ((tops, lo), (lows, hi)):
                    d = jnp.minimum(cft[rows] - ra[:, rows], rb[:, rows] - cet[rows])
                    d = jnp.exp(d).astype(BF16)
                    part.append(jnp.concatenate([gf_ref[rows, rows] * d, gr_ref[rows, rows] * d], axis=1))
            skip_row = jnp.where(first_half, skip[p * PER + 2 * pair], skip[p * PER + 2 * pair + 1])
            for part, rows, at in ((tops, lo, 0), (lows, hi, BLOCK)):
                res = dot(jnp.concatenate(part, axis=0), vcat[p, at : at + BLOCK, lanes])
                direct = skip_row * vcat[p, at : at + half, lanes].astype(F32)
                accw[p, rows, lanes] = direct + jnp.where(first_half, res[:half], res[half:])

    def y_copy(p):
        cols = pl.ds(pl.multiple_of(p * PIECE, PIECE), PIECE)
        return pltpu.make_async_copy(y_v.at[p], y_hbm.at[:, cols], out_sem.at[p])

    def finish(p):
        v = p // 4
        q = lax.rem(p, 4)
        cols = pl.ds(pl.multiple_of(p * PIECE, PIECE), PIECE)
        growf = dot(aft[v], sel[q, :, 2 * PIECE : 3 * PIECE])
        growr = dot(aft[v], sel[q, :, 3 * PIECE : 4 * PIECE])
        ef = cinf[p]
        er = cinr[p]
        late_f = (midf[p] + drow[p, 0:1, :] * ef.astype(F32)).astype(BF16)
        late_r = (midr[p] + drow[p, 1:2, :] * er.astype(F32)).astype(BF16)
        f = jnp.concatenate([dot(kq[1, lo, :], ef), dot(kq[1, hi, :], late_f)], axis=0)
        r = jnp.concatenate([dot(kq[3, lo, :], late_r), dot(kq[3, hi, :], er)], axis=0)
        gate = silu(gate_v[:, cols].astype(F32))
        y = (accw[p] + (growf * f + growr * r)) * gate
        y_v[p] = y.astype(BF16)
        y = y * y
        ssq[...] = ssq[...] + (y[:, :STATE] + y[:, STATE:])
        y_copy(p).start()

    ssq[...] = jnp.zeros_like(ssq)
    ready = jnp.maximum(PIECES + 1, 1 + LAG * jnp.maximum(me, n - 1 - me))

    def relays(k):
        for forward, late in ((True, 1 + LAG * me), (False, 1 + LAG * (n - 1 - me))):
            p = k - late

            @pl.when(jnp.logical_and(p >= 0, p < PIECES))
            def _():
                relay(p, forward)

    convolve(0)

    def slot_a(k, carry):
        states(k - 1)
        convolve(k)
        relays(k)
        return carry

    lax.fori_loop(1, PIECES, slot_a, 0)
    states(PIECES - 1)

    def slot_b(k, carry):
        relays(k)

        @pl.when(k >= ready)
        def _():
            finish(k - ready)
            within(k - PIECES)

        @pl.when(k < ready)
        def _():
            within(k - PIECES)

        return carry

    lax.fori_loop(PIECES, 2 * PIECES, slot_b, 0)

    def slot_c(k, carry):
        relays(k)

        @pl.when(k >= ready)
        def _():
            finish(k - ready)

        return carry

    lax.fori_loop(2 * PIECES, ready + PIECES, slot_c, 0)
    mean = jnp.sum(ssq[...], axis=1, keepdims=True) * (1.0 / INNER)
    scale_ref[...] = jnp.broadcast_to(lax.rsqrt(mean + 1e-05), scale_ref.shape)

    @pl.when(has_right)
    def _():
        def done(p, carry):
            hop(p, True).wait_send()
            return carry

        lax.fori_loop(0, PIECES, done, 0)

    @pl.when(has_left)
    def _():
        def done(p, carry):
            hop(p, False).wait_send()
            return carry

        lax.fori_loop(0, PIECES, done, 0)

    def stored(p, carry):
        y_copy(p).wait()
        return carry

    lax.fori_loop(0, PIECES, stored, 0)


def scale_rows(y_hbm, scale_ref, gain_ref, out_hbm, y_v, out_v, in_sem, out_sem):
    parts = [pl.ds(r, STRIP) for r in range(0, BLOCK, STRIP)]
    loads = [pltpu.make_async_copy(y_hbm.at[s], y_v.at[s], in_sem.at[i]) for i, s in enumerate(parts)]
    stores = [
        pltpu.make_async_copy(out_v.at[s], out_hbm.at[s], out_sem.at[i]) for i, s in enumerate(parts)
    ]
    for load in loads:
        load.start()
    for i, rows in enumerate(parts):
        loads[i].wait()
        scale = scale_ref[rows, :]
        for c in range(0, INNER, STATE):
            cols = pl.ds(c, STATE)
            out_v[rows, cols] = (y_v[rows, cols].astype(F32) * scale * gain_ref[:, cols]).astype(BF16)
        stores[i].start()
    for store in stores:
        store.wait()


def per_device(
    mixer_input, gate_input, conv_forward, conv_reverse, step_size, decay_rate, skip_scale, norm_gain
):
    n = lax.axis_size("seq")
    vmem = pl.BlockSpec(memory_space=pltpu.VMEM)
    smem = pl.BlockSpec(memory_space=pltpu.SMEM)
    hbm = pl.BlockSpec(memory_space=pl.ANY)
    piece = (PIECES, BLOCK, PIECE)
    state = (PIECES, STATE, PIECE)
    dma = pltpu.SemaphoreType.DMA
    y, scale = pl.pallas_call(
        functools.partial(kernel, n),
        out_shape=(
            jax.ShapeDtypeStruct((BLOCK, INNER), BF16),
            jax.ShapeDtypeStruct((BLOCK, STATE), F32),
        ),
        in_specs=[hbm, hbm, vmem, vmem, vmem, smem, smem],
        out_specs=(hbm, vmem),
        scratch_shapes=[
            pltpu.VMEM((BLOCK + 2 * HALO, INNER + 2 * STATE), BF16),
            pltpu.VMEM((BLOCK, INNER), BF16),
            pltpu.VMEM((PIECES, 2 * BLOCK, PIECE), BF16),
            pltpu.VMEM(piece, F32),
            pltpu.VMEM(state, F32),
            pltpu.VMEM(state, F32),
            pltpu.VMEM(state, F32),
            pltpu.VMEM(state, F32),
            pltpu.VMEM(state, BF16),
            pltpu.VMEM(state, BF16),
            pltpu.VMEM(state, BF16),
            pltpu.VMEM(state, BF16),
            pltpu.VMEM((PIECES, BLOCK, STATE), F32),
            pltpu.VMEM((HEADS, BLOCK), F32),
            pltpu.VMEM((HEADS, BLOCK), F32),
            pltpu.VMEM((PIECES, 2 * PER, BLOCK), F32),
            pltpu.VMEM((PIECES // 4, BLOCK, STATE), BF16),
            pltpu.VMEM((4, STATE, 4 * PIECE), BF16),
            pltpu.VMEM((PIECES, 8, PIECE), F32),
            pltpu.VMEM((BLOCK, BLOCK), BF16),
            pltpu.VMEM((BLOCK, BLOCK), BF16),
            pltpu.VMEM((4, BLOCK, STATE), BF16),
            pltpu.VMEM((2, STATE, BLOCK), BF16),
            pltpu.VMEM((BLOCK, STATE), F32),
            pltpu.VMEM(piece, BF16),
            pltpu.VMEM((BLOCK + 2 * HALO, STATE), F32),
            pltpu.VMEM((BLOCK + 2 * HALO, STATE), F32),
            dma((2,)),
            dma((2,)),
            dma((2,)),
            dma((PIECES,)),
            dma((PIECES,)),
            dma((PIECES,)),
            dma((PIECES,)),
            dma((PIECES,)),
        ],
        compiler_params=pltpu.CompilerParams(
            collective_id=0, has_side_effects=True, vmem_limit_bytes=56 * 1024 * 1024
        ),
        cost_estimate=pl.CostEstimate(flops=3 * 10**9, bytes_accessed=7 * 10**6, transcendentals=10**7),
        name="mixer",
    )(
        mixer_input, gate_input, conv_forward, conv_reverse, step_size, decay_rate, skip_scale
    )
    dma = pltpu.SemaphoreType.DMA
    parts = BLOCK // STRIP
    return pl.pallas_call(
        scale_rows,
        out_shape=jax.ShapeDtypeStruct((BLOCK, INNER), BF16),
        in_specs=[hbm, vmem, vmem],
        out_specs=hbm,
        scratch_shapes=[
            pltpu.VMEM((BLOCK, INNER), BF16),
            pltpu.VMEM((BLOCK, INNER), BF16),
            dma((parts,)),
            dma((parts,)),
        ],
        compiler_params=pltpu.CompilerParams(vmem_limit_bytes=60 * 1024 * 1024),
        cost_estimate=pl.CostEstimate(flops=2 * 10**6, bytes_accessed=4 * 10**6, transcendentals=0),
        name="scale_rows",
    )(y, scale, norm_gain.reshape(1, INNER))


def solution(mesh):
    in_specs = (
        P(("row", "seq"), None),
        P(("row", "seq"), None),
        P(),
        P(),
        P(None, ("row", "seq")),
        P("row"),
        P(),
        P(),
    )
    out_specs = P(("row", "seq"), None)
    return jax.shard_map(
        per_device, mesh=mesh, in_specs=in_specs, out_specs=out_specs, check_vma=False
    )
```

```python
import functools

import jax
import jax.numpy as jnp
from jax import lax
from jax.experimental import pallas as pl
from jax.experimental.pallas import tpu as pltpu
from jax.sharding import PartitionSpec as P

HEADS = 64
HEAD_DIM = 64
STATE = 128
WIDTH = 4
BLOCK = 256
INNER = HEADS * HEAD_DIM
PIECE = 256
PIECES = INNER // PIECE
PER = PIECE // HEAD_DIM
HALO = 16
STRIP = 64
LAG = 4
PAIR = 2
F32 = jnp.float32
BF16 = jnp.bfloat16
MESH = pl.DeviceIdType.MESH


def dot(a, b):
    return jnp.dot(a, b, preferred_element_type=F32)


def silu(x):
    y = 0.5 * x
    return y + y * jnp.tanh(y)


def kernel(
    n,
    x_hbm, gate_hbm, tapf, tapr, step_ref, decay, skip, y_hbm, scale_ref,
    xpad, gate_v, vcat, accw, st, midf, midr, chain_in, peer_in, ent, give, out_sb,
    colc, cfs, ces, rowc, aft, sel, drow, gf_ref, gr_ref, kq, kt, ssq, y_v, xf0, xf1,
    local_sem, halo_send, halo_recv,
    peer_send, peer_recv, chain_send, chain_recv, ent_send, ent_recv, out_sem,
):
    me = lax.axis_index("seq")
    has_left = me > 0
    has_right = me < n - 1
    left = lax.rem(me + n - 1, n)
    right = lax.rem(me + 1, n)

    load_x = pltpu.make_async_copy(x_hbm, xpad.at[pl.ds(HALO, BLOCK)], local_sem.at[0])
    load_gate = pltpu.make_async_copy(gate_hbm, gate_v, local_sem.at[1])
    load_x.start()
    load_gate.start()

    barrier = pltpu.get_barrier_semaphore()

    peers = jnp.int32(0)
    for d in (-1, 1, -2, 2):
        there = jnp.logical_and(me + d >= 0, me + d < n)
        peers = peers + there.astype(jnp.int32)

        @pl.when(there)
        def _():
            pl.semaphore_signal(
                barrier, inc=1, device_id={"seq": lax.rem(me + d + n, n)}, device_id_type=MESH
            )

    pl.semaphore_wait(barrier, peers)

    core = lax.rem(me, 2)
    chip = me // 2
    chips = n // 2
    mine = 1 - core
    other = core
    far_f = chip
    far_r = chips - 1 - chip
    far_mine = jnp.where(core == 1, far_f, far_r)
    far_other = jnp.where(core == 1, far_r, far_f)
    partner = me + 1 - 2 * core
    onward = lax.rem(me + 4 * core - 2 + n, n)
    takes = far_mine > 0
    gives = far_mine < chips - 1
    fed = far_other > 0

    to_right = pltpu.make_async_remote_copy(
        src_ref=x_hbm.at[pl.ds(BLOCK - HALO, HALO)],
        dst_ref=xpad.at[pl.ds(0, HALO)],
        send_sem=halo_send.at[0],
        recv_sem=halo_recv.at[0],
        device_id={"seq": right},
        device_id_type=MESH,
    )
    to_left = pltpu.make_async_remote_copy(
        src_ref=x_hbm.at[pl.ds(0, HALO)],
        dst_ref=xpad.at[pl.ds(HALO + BLOCK, HALO)],
        send_sem=halo_send.at[1],
        recv_sem=halo_recv.at[1],
        device_id={"seq": left},
        device_id_type=MESH,
    )

    @pl.when(has_right)
    def _():
        to_right.start()

    @pl.when(has_left)
    def _():
        to_left.start()

    @pl.when(jnp.logical_not(has_left))
    def _():
        xpad[0:HALO, :] = jnp.zeros((HALO, xpad.shape[1]), BF16)

    @pl.when(jnp.logical_not(has_right))
    def _():
        xpad[HALO + BLOCK :, :] = jnp.zeros((HALO, xpad.shape[1]), BF16)

    @pl.when(jnp.logical_not(takes))
    def _():
        chain_in[...] = jnp.zeros(chain_in.shape, BF16)

    @pl.when(jnp.logical_not(fed))
    def _():
        ent[other] = jnp.zeros(ent.shape[1:], BF16)

    half = BLOCK // 2
    lo, hi = slice(0, half), slice(half, BLOCK)
    for h in range(HEADS):
        ces[h : h + 1, :] = step_ref[h : h + 1, :] * (-decay[h])
    logs = ces[...]
    row_i = lax.broadcasted_iota(jnp.int32, (BLOCK, BLOCK), 0)
    col_i = lax.broadcasted_iota(jnp.int32, (BLOCK, BLOCK), 1)
    upto = jnp.where(row_i <= col_i, 1.0, 0.0).astype(F32)
    cum = jnp.dot(logs, upto, preferred_element_type=F32, precision=lax.Precision.HIGHEST)
    before = cum - logs
    total = cum[:, BLOCK - 1 : BLOCK]
    steps = step_ref[...]
    log_steps = jnp.log(steps)
    cfs[...] = cum - log_steps
    ces[...] = before + log_steps
    for p in range(PIECES):
        rowc[p, 0:PER, :] = cfs[p * PER : (p + 1) * PER, :]
        rowc[p, PER : 2 * PER, :] = ces[p * PER : (p + 1) * PER, :]
    columns = jnp.transpose(jnp.concatenate([cum, before], axis=0))
    for p in range(PIECES):
        shift = (STATE - PER * p) % STATE
        colc[p] = pltpu.roll(columns, shift, axis=1) if shift else columns
    middle = cum[:, half - 1 : half]
    early = lax.broadcasted_iota(jnp.int32, cum.shape, 1) < half
    start = jnp.where(early, 0.0, middle)
    end = jnp.where(early, middle, total)
    factors = (
        steps * jnp.exp(end - cum),
        steps * jnp.exp(before - start),
        jnp.exp(cum - start),
        jnp.exp(end - before),
    )
    parts = []
    for f in factors:
        high = f.astype(BF16).astype(F32)
        parts.append((high, f - high))
    for v in range(PIECES // 4):
        rows = []
        for u in (2 * v, 2 * v + 1):
            for high, low in parts:
                rows.append(high[8 * u : 8 * u + 8])
                rows.append(low[8 * u : 8 * u + 8])
        aft[v] = jnp.transpose(jnp.concatenate(rows, axis=0)).astype(BF16)
    sel_row = lax.broadcasted_iota(jnp.int32, (STATE, PIECE), 0)
    sel_col = lax.broadcasted_iota(jnp.int32, (STATE, PIECE), 1) >> 6
    base = sel_row - sel_col
    for q in range(4):
        for f in range(4):
            off = (q // 2) * 64 + f * 16 + (q % 2) * 4
            hit = jnp.logical_or(base == off, base == off + 8)
            sel[q, :, f * PIECE : (f + 1) * PIECE] = jnp.where(hit, 1.0, 0.0).astype(BF16)

    xfs = (xf0, xf1)
    load_x.wait()

    @pl.when(has_right)
    def _():
        to_right.wait_send()
        to_left.wait_recv()

    @pl.when(has_left)
    def _():
        to_right.wait_recv()
        to_left.wait_send()

    def conv(cols, xf):
        xf[...] = xpad[:, cols].astype(F32)
        fw = tapf[:, cols]
        rv = tapr[:, cols]
        for r in range(0, BLOCK, STRIP):
            ahead = behind = None
            for k in range(WIDTH):
                a = fw[k : k + 1] * xf[pl.ds(HALO + r + k - (WIDTH - 1), STRIP), :]
                b = rv[k : k + 1] * xf[pl.ds(HALO + r + WIDTH - 1 - k, STRIP), :]
                ahead = a if ahead is None else ahead + a
                behind = b if behind is None else behind + b
            yield r, silu(ahead).astype(BF16), silu(behind).astype(BF16)

    for which in range(2):
        for r, a, b in conv(pl.ds(INNER + which * STATE, STATE), xfs[which]):
            kq[which, r : r + STRIP, :] = a
            kq[2 + which, r : r + STRIP, :] = b
    for i in range(2):
        keys = jnp.transpose(kq[2 * i].astype(F32)).astype(BF16)
        kt[i] = keys
        inside = row_i >= col_i if i == 0 else row_i <= col_i
        (gf_ref, gr_ref)[i][...] = jnp.where(inside, dot(kq[2 * i + 1], keys), 0.0).astype(BF16)
    load_gate.wait()

    lane = lax.broadcasted_iota(jnp.int32, (1, STATE), 1)
    first_half = lane < HEAD_DIM

    def convolve(p):
        for c in range(PIECE // STATE):
            cols = pl.ds(pl.multiple_of(p * PIECE + c * STATE, STATE), STATE)
            for r, a, b in conv(cols, xfs[c]):
                at = r // half * BLOCK + r % half
                vcat[p, pl.ds(at, STRIP), pl.ds(c * STATE, STATE)] = a
                vcat[p, pl.ds(half + at, STRIP), pl.ds(c * STATE, STATE)] = b

    def states(p):
        v = p // 4
        q = lax.rem(p, 4)
        for i in range(2):
            ends = dot(aft[v, i * half + half - 16 : (i + 1) * half, :], sel[q, :, 2 * PIECE : 3 * PIECE])
            drow[p, i : i + 1, :] = ends[15:16, :]
        for i, mid in enumerate((midf, midr)):
            wide = dot(aft[v], sel[q, :, i * PIECE : (i + 1) * PIECE])
            top = i * half
            low = (vcat[p, top : top + half, :].astype(F32) * wide[lo]).astype(BF16)
            high = (vcat[p, BLOCK + top : BLOCK + top + half, :].astype(F32) * wide[hi]).astype(BF16)
            low = dot(kt[i, :, lo], low)
            high = dot(kt[i, :, hi], high)
            first, second = (low, high) if i == 0 else (high, low)
            mid[p] = first
            st[i, p] = second + drow[p, 1 - i : 2 - i, :] * first

        whole = drow[p, 0:1, :] * drow[p, 1:2, :]
        high = whole.astype(BF16).astype(F32)
        row = lax.broadcasted_iota(jnp.int32, (16, PIECE), 0)
        tail = jnp.where(row == 0, high, jnp.where(row == 1, whole - high, 0.0))
        give[p, 0:STATE, :] = st[other, p].astype(BF16)
        give[p, STATE:, :] = tail.astype(BF16)
        to_partner(p).start()

    def to_partner(p):
        return pltpu.make_async_remote_copy(
            src_ref=give.at[p],
            dst_ref=peer_in.at[p],
            send_sem=peer_send.at[p],
            recv_sem=peer_recv.at[p],
            device_id={"seq": partner},
            device_id_type=MESH,
        )

    def to_chip(p):
        return pltpu.make_async_remote_copy(
            src_ref=out_sb.at[p],
            dst_ref=chain_in.at[p],
            send_sem=chain_send.at[p],
            recv_sem=chain_recv.at[p],
            device_id={"seq": onward},
            device_id_type=MESH,
        )

    def to_entry(p):
        return pltpu.make_async_remote_copy(
            src_ref=chain_in.at[p],
            dst_ref=ent.at[mine, p],
            send_sem=ent_send.at[p],
            recv_sem=ent_recv.at[p],
            device_id={"seq": partner},
            device_id_type=MESH,
        )

    def relay(p):
        to_partner(p).wait_recv()

        @pl.when(takes)
        def _():
            to_chip(p).wait_recv()
            to_entry(p).start()

        beside = peer_in[p, STATE : STATE + 16, :].astype(F32)
        beside = beside[0:1] + beside[1:2]
        entry = peer_in[p, 0:STATE, :].astype(F32) + beside * chain_in[p].astype(F32)
        whole = drow[p, 0:1, :] * drow[p, 1:2, :]

        @pl.when(gives)
        def _():
            out_sb[p] = (st[mine, p] + whole * entry).astype(BF16)
            to_chip(p).start()

        ent[mine, p] = entry.astype(BF16)

    def within(p):
        for pair in range(PER // 2):
            lanes = slice(pair * STATE, (pair + 1) * STATE)
            tops, lows = [], []
            for j in (2 * pair, 2 * pair + 1):
                cft = jnp.broadcast_to(colc[p, :, j : j + 1], (BLOCK, half))
                cet = jnp.broadcast_to(colc[p, :, 64 + j : 65 + j], (BLOCK, half))
                ra = rowc[p, j : j + 1, :]
                rb = rowc[p, PER + j : PER + j + 1, :]
                for part, rows in ((tops, lo), (lows, hi)):
                    d = jnp.minimum(cft[rows] - ra[:, rows], rb[:, rows] - cet[rows])
                    d = jnp.exp(d).astype(BF16)
                    part.append(jnp.concatenate([gf_ref[rows, rows] * d, gr_ref[rows, rows] * d], axis=1))
            skip_row = jnp.where(first_half, skip[p * PER + 2 * pair], skip[p * PER + 2 * pair + 1])
            for part, rows, at in ((tops, lo, 0), (lows, hi, BLOCK)):
                res = dot(jnp.concatenate(part, axis=0), vcat[p, at : at + BLOCK, lanes])
                direct = skip_row * vcat[p, at : at + half, lanes].astype(F32)
                accw[p, rows, lanes] = direct + jnp.where(first_half, res[:half], res[half:])

    def y_copy(p):
        cols = pl.ds(pl.multiple_of(p * PIECE, PIECE), PIECE)
        return pltpu.make_async_copy(y_v.at[p], y_hbm.at[:, cols], out_sem.at[p])

    def finish(p):
        v = p // 4
        q = lax.rem(p, 4)
        cols = pl.ds(pl.multiple_of(p * PIECE, PIECE), PIECE)
        growf = dot(aft[v], sel[q, :, 2 * PIECE : 3 * PIECE])
        growr = dot(aft[v], sel[q, :, 3 * PIECE : 4 * PIECE])
        ef = ent[0, p]
        er = ent[1, p]
        late_f = (midf[p] + drow[p, 0:1, :] * ef.astype(F32)).astype(BF16)
        late_r = (midr[p] + drow[p, 1:2, :] * er.astype(F32)).astype(BF16)
        f = jnp.concatenate([dot(kq[1, lo, :], ef), dot(kq[1, hi, :], late_f)], axis=0)
        r = jnp.concatenate([dot(kq[3, lo, :], late_r), dot(kq[3, hi, :], er)], axis=0)
        gate = silu(gate_v[:, cols].astype(F32))
        y = (accw[p] + (growf * f + growr * r)) * gate
        y_v[p] = y.astype(BF16)
        y = y * y
        ssq[...] = ssq[...] + (y[:, :STATE] + y[:, STATE:])
        y_copy(p).start()

    ssq[...] = jnp.zeros_like(ssq)
    late = 1 + PAIR + LAG * far_mine
    ready = jnp.maximum(jnp.maximum(PIECES + 1, late), 1 + 2 * PAIR + LAG * far_other)

    def relays(k):
        @pl.when(jnp.logical_and(k >= late, k < late + PIECES))
        def _():
            relay(k - late)

        @pl.when(jnp.logical_and(jnp.logical_and(k >= ready, k < ready + PIECES), fed))
        def _():
            to_entry(k - ready).wait_recv()

    convolve(0)

    def slot_a(k, carry):
        states(k - 1)
        convolve(k)
        relays(k)
        return carry

    lax.fori_loop(1, PIECES, slot_a, 0)
    states(PIECES - 1)

    def slot_b(k, carry):
        relays(k)

        @pl.when(k >= ready)
        def _():
            finish(k - ready)
            within(k - PIECES)

        @pl.when(k < ready)
        def _():
            within(k - PIECES)

        return carry

    lax.fori_loop(PIECES, 2 * PIECES, slot_b, 0)

    def slot_c(k, carry):
        relays(k)

        @pl.when(k >= ready)
        def _():
            finish(k - ready)

        return carry

    lax.fori_loop(2 * PIECES, ready + PIECES, slot_c, 0)
    mean = jnp.sum(ssq[...], axis=1, keepdims=True) * (1.0 / INNER)
    scale_ref[...] = jnp.broadcast_to(lax.rsqrt(mean + 1e-05), scale_ref.shape)

    def done(p, carry):
        to_partner(p).wait_send()

        @pl.when(gives)
        def _():
            to_chip(p).wait_send()

        @pl.when(takes)
        def _():
            to_entry(p).wait_send()

        return carry

    lax.fori_loop(0, PIECES, done, 0)

    def stored(p, carry):
        y_copy(p).wait()
        return carry

    lax.fori_loop(0, PIECES, stored, 0)


def scale_rows(y_hbm, scale_ref, gain_ref, out_hbm, y_v, out_v, in_sem, out_sem):
    parts = [pl.ds(r, STRIP) for r in range(0, BLOCK, STRIP)]
    loads = [pltpu.make_async_copy(y_hbm.at[s], y_v.at[s], in_sem.at[i]) for i, s in enumerate(parts)]
    stores = [
        pltpu.make_async_copy(out_v.at[s], out_hbm.at[s], out_sem.at[i]) for i, s in enumerate(parts)
    ]
    for load in loads:
        load.start()
    for i, rows in enumerate(parts):
        loads[i].wait()
        scale = scale_ref[rows, :]
        for c in range(0, INNER, STATE):
            cols = pl.ds(c, STATE)
            out_v[rows, cols] = (y_v[rows, cols].astype(F32) * scale * gain_ref[:, cols]).astype(BF16)
        stores[i].start()
    for store in stores:
        store.wait()


def per_device(
    mixer_input, gate_input, conv_forward, conv_reverse, step_size, decay_rate, skip_scale, norm_gain
):
    n = lax.axis_size("seq")
    vmem = pl.BlockSpec(memory_space=pltpu.VMEM)
    smem = pl.BlockSpec(memory_space=pltpu.SMEM)
    hbm = pl.BlockSpec(memory_space=pl.ANY)
    piece = (PIECES, BLOCK, PIECE)
    state = (PIECES, STATE, PIECE)
    dma = pltpu.SemaphoreType.DMA
    y, scale = pl.pallas_call(
        functools.partial(kernel, n),
        out_shape=(
            jax.ShapeDtypeStruct((BLOCK, INNER), BF16),
            jax.ShapeDtypeStruct((BLOCK, STATE), F32),
        ),
        in_specs=[hbm, hbm, vmem, vmem, vmem, smem, smem],
        out_specs=(hbm, vmem),
        scratch_shapes=[
            pltpu.VMEM((BLOCK + 2 * HALO, INNER + 2 * STATE), BF16),
            pltpu.VMEM((BLOCK, INNER), BF16),
            pltpu.VMEM((PIECES, 2 * BLOCK, PIECE), BF16),
            pltpu.VMEM(piece, F32),
            pltpu.VMEM((2,) + state, F32),
            pltpu.VMEM(state, F32),
            pltpu.VMEM(state, F32),
            pltpu.VMEM(state, BF16),
            pltpu.VMEM((PIECES, STATE + 16, PIECE), BF16),
            pltpu.VMEM((2,) + state, BF16),
            pltpu.VMEM((PIECES, STATE + 16, PIECE), BF16),
            pltpu.VMEM(state, BF16),
            pltpu.VMEM((PIECES, BLOCK, STATE), F32),
            pltpu.VMEM((HEADS, BLOCK), F32),
            pltpu.VMEM((HEADS, BLOCK), F32),
            pltpu.VMEM((PIECES, 2 * PER, BLOCK), F32),
            pltpu.VMEM((PIECES // 4, BLOCK, STATE), BF16),
            pltpu.VMEM((4, STATE, 4 * PIECE), BF16),
            pltpu.VMEM((PIECES, 8, PIECE), F32),
            pltpu.VMEM((BLOCK, BLOCK), BF16),
            pltpu.VMEM((BLOCK, BLOCK), BF16),
            pltpu.VMEM((4, BLOCK, STATE), BF16),
            pltpu.VMEM((2, STATE, BLOCK), BF16),
            pltpu.VMEM((BLOCK, STATE), F32),
            pltpu.VMEM(piece, BF16),
            pltpu.VMEM((BLOCK + 2 * HALO, STATE), F32),
            pltpu.VMEM((BLOCK + 2 * HALO, STATE), F32),
            dma((2,)),
            dma((2,)),
            dma((2,)),
            dma((PIECES,)),
            dma((PIECES,)),
            dma((PIECES,)),
            dma((PIECES,)),
            dma((PIECES,)),
            dma((PIECES,)),
            dma((PIECES,)),
        ],
        compiler_params=pltpu.CompilerParams(
            collective_id=0, has_side_effects=True, vmem_limit_bytes=56 * 1024 * 1024
        ),
        cost_estimate=pl.CostEstimate(flops=3 * 10**9, bytes_accessed=7 * 10**6, transcendentals=10**7),
        name="mixer",
    )(
        mixer_input, gate_input, conv_forward, conv_reverse, step_size, decay_rate, skip_scale
    )
    dma = pltpu.SemaphoreType.DMA
    parts = BLOCK // STRIP
    return pl.pallas_call(
        scale_rows,
        out_shape=jax.ShapeDtypeStruct((BLOCK, INNER), BF16),
        in_specs=[hbm, vmem, vmem],
        out_specs=hbm,
        scratch_shapes=[
            pltpu.VMEM((BLOCK, INNER), BF16),
            pltpu.VMEM((BLOCK, INNER), BF16),
            dma((parts,)),
            dma((parts,)),
        ],
        compiler_params=pltpu.CompilerParams(vmem_limit_bytes=60 * 1024 * 1024),
        cost_estimate=pl.CostEstimate(flops=2 * 10**6, bytes_accessed=4 * 10**6, transcendentals=0),
        name="scale_rows",
    )(y, scale, norm_gain.reshape(1, INNER))


def solution(mesh):
    in_specs = (
        P(("row", "seq"), None),
        P(("row", "seq"), None),
        P(),
        P(),
        P(None, ("row", "seq")),
        P("row"),
        P(),
        P(),
    )
    out_specs = P(("row", "seq"), None)
    return jax.shard_map(
        per_device, mesh=mesh, in_specs=in_specs, out_specs=out_specs, check_vma=False
    )
```

```python
import functools

import jax
import jax.numpy as jnp
from jax import lax
from jax.experimental import pallas as pl
from jax.experimental.pallas import tpu as pltpu
from jax.sharding import PartitionSpec as P

HEADS = 64
HEAD_DIM = 64
STATE = 128
WIDTH = 4
BLOCK = 256
INNER = HEADS * HEAD_DIM
PIECE = 256
PIECES = INNER // PIECE
PER = PIECE // HEAD_DIM
HALO = 16
STRIP = 64
LAG = 4
PAIR = 3
F32 = jnp.float32
BF16 = jnp.bfloat16
MESH = pl.DeviceIdType.MESH


def dot(a, b):
    return jnp.dot(a, b, preferred_element_type=F32)


def silu(x):
    y = 0.5 * x
    return y + y * jnp.tanh(y)


def kernel(
    n,
    x_hbm, gate_hbm, tapf_hbm, tapr_hbm, step_hbm, decay, skip, y_hbm, scale_ref,
    tapf, tapr, step_ref, xpad, gate_v, vcat, accw, st, midf, midr, chain_in, peer_in, ent, give, out_sb,
    colc, cfs, ces, rowc, aft, sel, drow, gf_ref, gr_ref, kq, kt, ssq, y_v, xf0, xf1,
    local_sem, halo_send, halo_recv,
    peer_send, peer_recv, chain_send, chain_recv, ent_send, ent_recv, out_sem,
):
    me = lax.axis_index("seq")
    has_left = me > 0
    has_right = me < n - 1
    left = lax.rem(me + n - 1, n)
    right = lax.rem(me + 1, n)

    load_x = pltpu.make_async_copy(x_hbm, xpad.at[pl.ds(HALO, BLOCK)], local_sem.at[0])
    load_gate = pltpu.make_async_copy(gate_hbm, gate_v, local_sem.at[1])
    load_step = pltpu.make_async_copy(step_hbm, step_ref, local_sem.at[2])
    load_tapf = pltpu.make_async_copy(tapf_hbm, tapf, local_sem.at[3])
    load_tapr = pltpu.make_async_copy(tapr_hbm, tapr, local_sem.at[4])
    load_step.start()
    load_tapf.start()
    load_tapr.start()
    load_x.start()
    load_gate.start()

    barrier = pltpu.get_barrier_semaphore()

    peers = jnp.int32(0)
    for d in (-1, 1, -2, 2):
        there = jnp.logical_and(me + d >= 0, me + d < n)
        peers = peers + there.astype(jnp.int32)

        @pl.when(there)
        def _():
            pl.semaphore_signal(
                barrier, inc=1, device_id={"seq": lax.rem(me + d + n, n)}, device_id_type=MESH
            )

    pl.semaphore_wait(barrier, peers)

    core = lax.rem(me, 2)
    chip = me // 2
    chips = n // 2
    mine = 1 - core
    other = core
    far_f = chip
    far_r = chips - 1 - chip
    far_mine = jnp.where(core == 1, far_f, far_r)
    far_other = jnp.where(core == 1, far_r, far_f)
    partner = me + 1 - 2 * core
    onward = lax.rem(me + 4 * core - 2 + n, n)
    takes = far_mine > 0
    gives = far_mine < chips - 1
    fed = far_other > 0

    to_right = pltpu.make_async_remote_copy(
        src_ref=x_hbm.at[pl.ds(BLOCK - HALO, HALO)],
        dst_ref=xpad.at[pl.ds(0, HALO)],
        send_sem=halo_send.at[0],
        recv_sem=halo_recv.at[0],
        device_id={"seq": right},
        device_id_type=MESH,
    )
    to_left = pltpu.make_async_remote_copy(
        src_ref=x_hbm.at[pl.ds(0, HALO)],
        dst_ref=xpad.at[pl.ds(HALO + BLOCK, HALO)],
        send_sem=halo_send.at[1],
        recv_sem=halo_recv.at[1],
        device_id={"seq": left},
        device_id_type=MESH,
    )

    @pl.when(has_right)
    def _():
        to_right.start()

    @pl.when(has_left)
    def _():
        to_left.start()

    @pl.when(jnp.logical_not(has_left))
    def _():
        xpad[0:HALO, :] = jnp.zeros((HALO, xpad.shape[1]), BF16)

    @pl.when(jnp.logical_not(has_right))
    def _():
        xpad[HALO + BLOCK :, :] = jnp.zeros((HALO, xpad.shape[1]), BF16)

    @pl.when(jnp.logical_not(takes))
    def _():
        chain_in[...] = jnp.zeros(chain_in.shape, BF16)

    @pl.when(jnp.logical_not(fed))
    def _():
        ent[other] = jnp.zeros(ent.shape[1:], BF16)

    half = BLOCK // 2
    lo, hi = slice(0, half), slice(half, BLOCK)
    load_step.wait()
    for h in range(HEADS):
        ces[h : h + 1, :] = step_ref[h : h + 1, :] * (-decay[h])
    logs = ces[...]
    row_i = lax.broadcasted_iota(jnp.int32, (BLOCK, BLOCK), 0)
    col_i = lax.broadcasted_iota(jnp.int32, (BLOCK, BLOCK), 1)
    upto = jnp.where(row_i <= col_i, 1.0, 0.0).astype(F32)
    cum = jnp.dot(logs, upto, preferred_element_type=F32, precision=lax.Precision.HIGHEST)
    before = cum - logs
    total = cum[:, BLOCK - 1 : BLOCK]
    steps = step_ref[...]
    log_steps = jnp.log(steps)
    cfs[...] = cum - log_steps
    ces[...] = before + log_steps
    for p in range(PIECES):
        rowc[p, 0:PER, :] = cfs[p * PER : (p + 1) * PER, :]
        rowc[p, PER : 2 * PER, :] = ces[p * PER : (p + 1) * PER, :]
    columns = jnp.transpose(jnp.concatenate([cum, before], axis=0))
    for p in range(PIECES):
        shift = (STATE - PER * p) % STATE
        colc[p] = pltpu.roll(columns, shift, axis=1) if shift else columns
    middle = cum[:, half - 1 : half]
    early = lax.broadcasted_iota(jnp.int32, cum.shape, 1) < half
    start = jnp.where(early, 0.0, middle)
    end = jnp.where(early, middle, total)
    factors = (
        steps * jnp.exp(end - cum),
        steps * jnp.exp(before - start),
        jnp.exp(cum - start),
        jnp.exp(end - before),
    )
    parts = []
    for f in factors:
        high = f.astype(BF16).astype(F32)
        parts.append((high, f - high))
    for v in range(PIECES // 4):
        rows = []
        for u in (2 * v, 2 * v + 1):
            for high, low in parts:
                rows.append(high[8 * u : 8 * u + 8])
                rows.append(low[8 * u : 8 * u + 8])
        aft[v] = jnp.transpose(jnp.concatenate(rows, axis=0)).astype(BF16)
    sel_row = lax.broadcasted_iota(jnp.int32, (STATE, PIECE), 0)
    sel_col = lax.broadcasted_iota(jnp.int32, (STATE, PIECE), 1) >> 6
    base = sel_row - sel_col
    for q in range(4):
        for f in range(4):
            off = (q // 2) * 64 + f * 16 + (q % 2) * 4
            hit = jnp.logical_or(base == off, base == off + 8)
            sel[q, :, f * PIECE : (f + 1) * PIECE] = jnp.where(hit, 1.0, 0.0).astype(BF16)

    xfs = (xf0, xf1)
    load_x.wait()
    load_tapf.wait()
    load_tapr.wait()

    @pl.when(has_right)
    def _():
        to_right.wait_send()
        to_left.wait_recv()

    @pl.when(has_left)
    def _():
        to_right.wait_recv()
        to_left.wait_send()

    def conv(cols, xf):
        xf[...] = xpad[:, cols].astype(F32)
        fw = tapf[:, cols]
        rv = tapr[:, cols]
        for r in range(0, BLOCK, STRIP):
            ahead = behind = None
            for k in range(WIDTH):
                a = fw[k : k + 1] * xf[pl.ds(HALO + r + k - (WIDTH - 1), STRIP), :]
                b = rv[k : k + 1] * xf[pl.ds(HALO + r + WIDTH - 1 - k, STRIP), :]
                ahead = a if ahead is None else ahead + a
                behind = b if behind is None else behind + b
            yield r, silu(ahead).astype(BF16), silu(behind).astype(BF16)

    for which in range(2):
        for r, a, b in conv(pl.ds(INNER + which * STATE, STATE), xfs[which]):
            kq[which, r : r + STRIP, :] = a
            kq[2 + which, r : r + STRIP, :] = b
    for i in range(2):
        keys = jnp.transpose(kq[2 * i].astype(F32)).astype(BF16)
        kt[i] = keys
        inside = row_i >= col_i if i == 0 else row_i <= col_i
        (gf_ref, gr_ref)[i][...] = jnp.where(inside, dot(kq[2 * i + 1], keys), 0.0).astype(BF16)
    load_gate.wait()

    lane = lax.broadcasted_iota(jnp.int32, (1, STATE), 1)
    first_half = lane < HEAD_DIM

    def convolve(p):
        for c in range(PIECE // STATE):
            cols = pl.ds(pl.multiple_of(p * PIECE + c * STATE, STATE), STATE)
            for r, a, b in conv(cols, xfs[c]):
                at = r // half * BLOCK + r % half
                vcat[p, pl.ds(at, STRIP), pl.ds(c * STATE, STATE)] = a
                vcat[p, pl.ds(half + at, STRIP), pl.ds(c * STATE, STATE)] = b

    def states(p):
        v = p // 4
        q = lax.rem(p, 4)
        for i in range(2):
            ends = dot(aft[v, i * half + half - 16 : (i + 1) * half, :], sel[q, :, 2 * PIECE : 3 * PIECE])
            drow[p, i : i + 1, :] = ends[15:16, :]
        for i, mid in enumerate((midf, midr)):
            wide = dot(aft[v], sel[q, :, i * PIECE : (i + 1) * PIECE])
            top = i * half
            low = (vcat[p, top : top + half, :].astype(F32) * wide[lo]).astype(BF16)
            high = (vcat[p, BLOCK + top : BLOCK + top + half, :].astype(F32) * wide[hi]).astype(BF16)
            low = dot(kt[i, :, lo], low)
            high = dot(kt[i, :, hi], high)
            first, second = (low, high) if i == 0 else (high, low)
            mid[p] = first
            st[i, p] = second + drow[p, 1 - i : 2 - i, :] * first

        whole = drow[p, 0:1, :] * drow[p, 1:2, :]
        high = whole.astype(BF16).astype(F32)
        row = lax.broadcasted_iota(jnp.int32, (16, PIECE), 0)
        tail = jnp.where(row == 0, high, jnp.where(row == 1, whole - high, 0.0))
        give[p, 0:STATE, :] = st[other, p].astype(BF16)
        give[p, STATE:, :] = tail.astype(BF16)
        to_partner(p).start()

    def to_partner(p):
        return pltpu.make_async_remote_copy(
            src_ref=give.at[p],
            dst_ref=peer_in.at[p],
            send_sem=peer_send.at[p],
            recv_sem=peer_recv.at[p],
            device_id={"seq": partner},
            device_id_type=MESH,
        )

    def to_chip(p):
        return pltpu.make_async_remote_copy(
            src_ref=out_sb.at[p],
            dst_ref=chain_in.at[p],
            send_sem=chain_send.at[p],
            recv_sem=chain_recv.at[p],
            device_id={"seq": onward},
            device_id_type=MESH,
        )

    def to_entry(p):
        return pltpu.make_async_remote_copy(
            src_ref=chain_in.at[p],
            dst_ref=ent.at[mine, p],
            send_sem=ent_send.at[p],
            recv_sem=ent_recv.at[p],
            device_id={"seq": partner},
            device_id_type=MESH,
        )

    def relay(p):
        to_partner(p).wait_recv()

        @pl.when(takes)
        def _():
            to_chip(p).wait_recv()
            to_entry(p).start()

        beside = peer_in[p, STATE : STATE + 16, :].astype(F32)
        beside = beside[0:1] + beside[1:2]
        entry = peer_in[p, 0:STATE, :].astype(F32) + beside * chain_in[p].astype(F32)
        whole = drow[p, 0:1, :] * drow[p, 1:2, :]

        @pl.when(gives)
        def _():
            out_sb[p] = (st[mine, p] + whole * entry).astype(BF16)
            to_chip(p).start()

        ent[mine, p] = entry.astype(BF16)

    def within(p):
        for pair in range(PER // 2):
            lanes = slice(pair * STATE, (pair + 1) * STATE)
            tops, lows = [], []
            for j in (2 * pair, 2 * pair + 1):
                cft = jnp.broadcast_to(colc[p, :, j : j + 1], (BLOCK, half))
                cet = jnp.broadcast_to(colc[p, :, 64 + j : 65 + j], (BLOCK, half))
                ra = rowc[p, j : j + 1, :]
                rb = rowc[p, PER + j : PER + j + 1, :]
                for part, rows in ((tops, lo), (lows, hi)):
                    d = jnp.minimum(cft[rows] - ra[:, rows], rb[:, rows] - cet[rows])
                    d = jnp.exp(d).astype(BF16)
                    part.append(jnp.concatenate([gf_ref[rows, rows] * d, gr_ref[rows, rows] * d], axis=1))
            skip_row = jnp.where(first_half, skip[p * PER + 2 * pair], skip[p * PER + 2 * pair + 1])
            for part, rows, at in ((tops, lo, 0), (lows, hi, BLOCK)):
                res = dot(jnp.concatenate(part, axis=0), vcat[p, at : at + BLOCK, lanes])
                direct = skip_row * vcat[p, at : at + half, lanes].astype(F32)
                accw[p, rows, lanes] = direct + jnp.where(first_half, res[:half], res[half:])

    def y_copy(p):
        cols = pl.ds(pl.multiple_of(p * PIECE, PIECE), PIECE)
        return pltpu.make_async_copy(y_v.at[p], y_hbm.at[:, cols], out_sem.at[p])

    def finish(p):
        v = p // 4
        q = lax.rem(p, 4)
        cols = pl.ds(pl.multiple_of(p * PIECE, PIECE), PIECE)
        growf = dot(aft[v], sel[q, :, 2 * PIECE : 3 * PIECE])
        growr = dot(aft[v], sel[q, :, 3 * PIECE : 4 * PIECE])
        ef = ent[0, p]
        er = ent[1, p]
        late_f = (midf[p] + drow[p, 0:1, :] * ef.astype(F32)).astype(BF16)
        late_r = (midr[p] + drow[p, 1:2, :] * er.astype(F32)).astype(BF16)
        f = jnp.concatenate([dot(kq[1, lo, :], ef), dot(kq[1, hi, :], late_f)], axis=0)
        r = jnp.concatenate([dot(kq[3, lo, :], late_r), dot(kq[3, hi, :], er)], axis=0)
        gate = silu(gate_v[:, cols].astype(F32))
        y = (accw[p] + (growf * f + growr * r)) * gate
        y_v[p] = y.astype(BF16)
        y = y * y
        ssq[...] = ssq[...] + (y[:, :STATE] + y[:, STATE:])
        y_copy(p).start()

    ssq[...] = jnp.zeros_like(ssq)
    late = 1 + PAIR + LAG * far_mine
    ready = jnp.maximum(jnp.maximum(PIECES + 1, late), 1 + 2 * PAIR + LAG * far_other)

    def relays(k):
        @pl.when(jnp.logical_and(k >= late, k < late + PIECES))
        def _():
            relay(k - late)

        @pl.when(jnp.logical_and(jnp.logical_and(k >= ready, k < ready + PIECES), fed))
        def _():
            to_entry(k - ready).wait_recv()

    convolve(0)

    def slot_a(k, carry):
        states(k - 1)
        convolve(k)
        relays(k)
        return carry

    lax.fori_loop(1, PIECES, slot_a, 0)
    states(PIECES - 1)

    def slot_b(k, carry):
        relays(k)

        @pl.when(k >= ready)
        def _():
            finish(k - ready)
            within(k - PIECES)

        @pl.when(k < ready)
        def _():
            within(k - PIECES)

        return carry

    lax.fori_loop(PIECES, 2 * PIECES, slot_b, 0)

    def slot_c(k, carry):
        relays(k)

        @pl.when(k >= ready)
        def _():
            finish(k - ready)

        return carry

    lax.fori_loop(2 * PIECES, ready + PIECES, slot_c, 0)
    mean = jnp.sum(ssq[...], axis=1, keepdims=True) * (1.0 / INNER)
    scale_ref[...] = jnp.broadcast_to(lax.rsqrt(mean + 1e-05), scale_ref.shape)

    def done(p, carry):
        to_partner(p).wait_send()

        @pl.when(gives)
        def _():
            to_chip(p).wait_send()

        @pl.when(takes)
        def _():
            to_entry(p).wait_send()

        return carry

    lax.fori_loop(0, PIECES, done, 0)

    def stored(p, carry):
        y_copy(p).wait()
        return carry

    lax.fori_loop(0, PIECES, stored, 0)


def scale_rows(y_hbm, scale_ref, gain_ref, out_hbm, y_v, out_v, in_sem, out_sem):
    parts = [pl.ds(r, STRIP) for r in range(0, BLOCK, STRIP)]
    loads = [pltpu.make_async_copy(y_hbm.at[s], y_v.at[s], in_sem.at[i]) for i, s in enumerate(parts)]
    stores = [
        pltpu.make_async_copy(out_v.at[s], out_hbm.at[s], out_sem.at[i]) for i, s in enumerate(parts)
    ]
    for load in loads:
        load.start()
    for i, rows in enumerate(parts):
        loads[i].wait()
        scale = scale_ref[rows, :]
        for c in range(0, INNER, STATE):
            cols = pl.ds(c, STATE)
            out_v[rows, cols] = (y_v[rows, cols].astype(F32) * scale * gain_ref[:, cols]).astype(BF16)
        stores[i].start()
    for store in stores:
        store.wait()


def per_device(
    mixer_input, gate_input, conv_forward, conv_reverse, step_size, decay_rate, skip_scale, norm_gain
):
    n = lax.axis_size("seq")
    vmem = pl.BlockSpec(memory_space=pltpu.VMEM)
    smem = pl.BlockSpec(memory_space=pltpu.SMEM)
    hbm = pl.BlockSpec(memory_space=pl.ANY)
    piece = (PIECES, BLOCK, PIECE)
    state = (PIECES, STATE, PIECE)
    dma = pltpu.SemaphoreType.DMA
    y, scale = pl.pallas_call(
        functools.partial(kernel, n),
        out_shape=(
            jax.ShapeDtypeStruct((BLOCK, INNER), BF16),
            jax.ShapeDtypeStruct((BLOCK, STATE), F32),
        ),
        in_specs=[hbm, hbm, hbm, hbm, hbm, smem, smem],
        out_specs=(hbm, vmem),
        scratch_shapes=[
            pltpu.VMEM((WIDTH, INNER + 2 * STATE), F32),
            pltpu.VMEM((WIDTH, INNER + 2 * STATE), F32),
            pltpu.VMEM((HEADS, BLOCK), F32),
            pltpu.VMEM((BLOCK + 2 * HALO, INNER + 2 * STATE), BF16),
            pltpu.VMEM((BLOCK, INNER), BF16),
            pltpu.VMEM((PIECES, 2 * BLOCK, PIECE), BF16),
            pltpu.VMEM(piece, F32),
            pltpu.VMEM((2,) + state, F32),
            pltpu.VMEM(state, F32),
            pltpu.VMEM(state, F32),
            pltpu.VMEM(state, BF16),
            pltpu.VMEM((PIECES, STATE + 16, PIECE), BF16),
            pltpu.VMEM((2,) + state, BF16),
            pltpu.VMEM((PIECES, STATE + 16, PIECE), BF16),
            pltpu.VMEM(state, BF16),
            pltpu.VMEM((PIECES, BLOCK, STATE), F32),
            pltpu.VMEM((HEADS, BLOCK), F32),
            pltpu.VMEM((HEADS, BLOCK), F32),
            pltpu.VMEM((PIECES, 2 * PER, BLOCK), F32),
            pltpu.VMEM((PIECES // 4, BLOCK, STATE), BF16),
            pltpu.VMEM((4, STATE, 4 * PIECE), BF16),
            pltpu.VMEM((PIECES, 8, PIECE), F32),
            pltpu.VMEM((BLOCK, BLOCK), BF16),
            pltpu.VMEM((BLOCK, BLOCK), BF16),
            pltpu.VMEM((4, BLOCK, STATE), BF16),
            pltpu.VMEM((2, STATE, BLOCK), BF16),
            pltpu.VMEM((BLOCK, STATE), F32),
            pltpu.VMEM(piece, BF16),
            pltpu.VMEM((BLOCK + 2 * HALO, STATE), F32),
            pltpu.VMEM((BLOCK + 2 * HALO, STATE), F32),
            dma((5,)),
            dma((2,)),
            dma((2,)),
            dma((PIECES,)),
            dma((PIECES,)),
            dma((PIECES,)),
            dma((PIECES,)),
            dma((PIECES,)),
            dma((PIECES,)),
            dma((PIECES,)),
        ],
        compiler_params=pltpu.CompilerParams(
            collective_id=0, has_side_effects=True, vmem_limit_bytes=56 * 1024 * 1024
        ),
        cost_estimate=pl.CostEstimate(flops=3 * 10**9, bytes_accessed=7 * 10**6, transcendentals=10**7),
        name="mixer",
    )(
        mixer_input, gate_input, conv_forward, conv_reverse, step_size, decay_rate, skip_scale
    )
    dma = pltpu.SemaphoreType.DMA
    parts = BLOCK // STRIP
    return pl.pallas_call(
        scale_rows,
        out_shape=jax.ShapeDtypeStruct((BLOCK, INNER), BF16),
        in_specs=[hbm, vmem, vmem],
        out_specs=hbm,
        scratch_shapes=[
            pltpu.VMEM((BLOCK, INNER), BF16),
            pltpu.VMEM((BLOCK, INNER), BF16),
            dma((parts,)),
            dma((parts,)),
        ],
        compiler_params=pltpu.CompilerParams(vmem_limit_bytes=60 * 1024 * 1024),
        cost_estimate=pl.CostEstimate(flops=2 * 10**6, bytes_accessed=4 * 10**6, transcendentals=0),
        name="scale_rows",
    )(y, scale, norm_gain.reshape(1, INNER))


def solution(mesh):
    in_specs = (
        P(("row", "seq"), None),
        P(("row", "seq"), None),
        P(),
        P(),
        P(None, ("row", "seq")),
        P("row"),
        P(),
        P(),
    )
    out_specs = P(("row", "seq"), None)
    return jax.shard_map(
        per_device, mesh=mesh, in_specs=in_specs, out_specs=out_specs, check_vma=False
    )
```

```python
import functools

import jax
import jax.numpy as jnp
from jax import lax
from jax.experimental import pallas as pl
from jax.experimental.pallas import tpu as pltpu
from jax.sharding import PartitionSpec as P

HEADS = 64
HEAD_DIM = 64
STATE = 128
WIDTH = 4
BLOCK = 256
INNER = HEADS * HEAD_DIM
PIECE = 256
PIECES = INNER // PIECE
PER = PIECE // HEAD_DIM
HALO = 16
STRIP = 64
TAIL = 32
LAG = 4
PAIR = 3
F32 = jnp.float32
BF16 = jnp.bfloat16
MESH = pl.DeviceIdType.MESH


def dot(a, b):
    return jnp.dot(a, b, preferred_element_type=F32)


def silu(x):
    y = 0.5 * x
    return y + y * jnp.tanh(y)


def kernel(
    n,
    x_hbm, gate_hbm, tapf_hbm, tapr_hbm, step_hbm, decay, skip, y_hbm, scale_ref,
    tapf, tapr, step_ref, xpad, gate_v, vcat, accw, st, midf, midr, chain_in, peer_in, ent, give, out_sb,
    colc, cfs, ces, rowc, aft, sel, drow, gf_ref, gr_ref, kq, kt, ssq, y_v, xf0, xf1,
    local_sem, halo_send, halo_recv,
    peer_send, peer_recv, chain_send, chain_recv, ent_send, ent_recv, out_sem,
):
    me = lax.axis_index("seq")
    has_left = me > 0
    has_right = me < n - 1
    left = lax.rem(me + n - 1, n)
    right = lax.rem(me + 1, n)

    load_x = pltpu.make_async_copy(x_hbm, xpad.at[pl.ds(HALO, BLOCK)], local_sem.at[0])
    load_gate = pltpu.make_async_copy(gate_hbm, gate_v, local_sem.at[1])
    load_step = pltpu.make_async_copy(step_hbm, step_ref, local_sem.at[2])
    load_tapf = pltpu.make_async_copy(tapf_hbm, tapf, local_sem.at[3])
    load_tapr = pltpu.make_async_copy(tapr_hbm, tapr, local_sem.at[4])
    load_step.start()
    load_tapf.start()
    load_tapr.start()
    load_x.start()
    load_gate.start()

    barrier = pltpu.get_barrier_semaphore()

    peers = jnp.int32(0)
    for d in (-1, 1, -2, 2):
        there = jnp.logical_and(me + d >= 0, me + d < n)
        peers = peers + there.astype(jnp.int32)

        @pl.when(there)
        def _():
            pl.semaphore_signal(
                barrier, inc=1, device_id={"seq": lax.rem(me + d + n, n)}, device_id_type=MESH
            )

    pl.semaphore_wait(barrier, peers)

    core = lax.rem(me, 2)
    chip = me // 2
    chips = n // 2
    mine = 1 - core
    other = core
    far_f = chip
    far_r = chips - 1 - chip
    far_mine = jnp.where(core == 1, far_f, far_r)
    far_other = jnp.where(core == 1, far_r, far_f)
    partner = me + 1 - 2 * core
    onward = lax.rem(me + 4 * core - 2 + n, n)
    takes = far_mine > 0
    gives = far_mine < chips - 1
    fed = far_other > 0

    to_right = pltpu.make_async_remote_copy(
        src_ref=x_hbm.at[pl.ds(BLOCK - HALO, HALO)],
        dst_ref=xpad.at[pl.ds(0, HALO)],
        send_sem=halo_send.at[0],
        recv_sem=halo_recv.at[0],
        device_id={"seq": right},
        device_id_type=MESH,
    )
    to_left = pltpu.make_async_remote_copy(
        src_ref=x_hbm.at[pl.ds(0, HALO)],
        dst_ref=xpad.at[pl.ds(HALO + BLOCK, HALO)],
        send_sem=halo_send.at[1],
        recv_sem=halo_recv.at[1],
        device_id={"seq": left},
        device_id_type=MESH,
    )

    @pl.when(has_right)
    def _():
        to_right.start()

    @pl.when(has_left)
    def _():
        to_left.start()

    @pl.when(jnp.logical_not(has_left))
    def _():
        xpad[0:HALO, :] = jnp.zeros((HALO, xpad.shape[1]), BF16)

    @pl.when(jnp.logical_not(has_right))
    def _():
        xpad[HALO + BLOCK :, :] = jnp.zeros((HALO, xpad.shape[1]), BF16)

    @pl.when(jnp.logical_not(takes))
    def _():
        chain_in[...] = jnp.zeros(chain_in.shape, BF16)

    @pl.when(jnp.logical_not(fed))
    def _():
        ent[other] = jnp.zeros(ent.shape[1:], BF16)

    half = BLOCK // 2
    lo, hi = slice(0, half), slice(half, BLOCK)
    load_step.wait()
    for h in range(HEADS):
        ces[h : h + 1, :] = step_ref[h : h + 1, :] * (-decay[h])
    logs = ces[...]
    row_i = lax.broadcasted_iota(jnp.int32, (BLOCK, BLOCK), 0)
    col_i = lax.broadcasted_iota(jnp.int32, (BLOCK, BLOCK), 1)
    upto = jnp.where(row_i <= col_i, 1.0, 0.0).astype(F32)
    cum = jnp.dot(logs, upto, preferred_element_type=F32, precision=lax.Precision.HIGHEST)
    before = cum - logs
    total = cum[:, BLOCK - 1 : BLOCK]
    steps = step_ref[...]
    log_steps = jnp.log(steps)
    cfs[...] = cum - log_steps
    ces[...] = before + log_steps
    for p in range(PIECES):
        rowc[p, 0:PER, :] = cfs[p * PER : (p + 1) * PER, :]
        rowc[p, PER : 2 * PER, :] = ces[p * PER : (p + 1) * PER, :]
    columns = jnp.transpose(jnp.concatenate([cum, before], axis=0))
    for p in range(PIECES):
        shift = (STATE - PER * p) % STATE
        colc[p] = pltpu.roll(columns, shift, axis=1) if shift else columns
    middle = cum[:, half - 1 : half]
    early = lax.broadcasted_iota(jnp.int32, cum.shape, 1) < half
    start = jnp.where(early, 0.0, middle)
    end = jnp.where(early, middle, total)
    factors = (
        steps * jnp.exp(end - cum),
        steps * jnp.exp(before - start),
        jnp.exp(cum - start),
        jnp.exp(end - before),
    )
    parts = []
    for f in factors:
        high = f.astype(BF16).astype(F32)
        parts.append((high, f - high))
    for v in range(PIECES // 4):
        rows = []
        for u in (2 * v, 2 * v + 1):
            for high, low in parts:
                rows.append(high[8 * u : 8 * u + 8])
                rows.append(low[8 * u : 8 * u + 8])
        aft[v] = jnp.transpose(jnp.concatenate(rows, axis=0)).astype(BF16)
    sel_row = lax.broadcasted_iota(jnp.int32, (STATE, PIECE), 0)
    sel_col = lax.broadcasted_iota(jnp.int32, (STATE, PIECE), 1) >> 6
    base = sel_row - sel_col
    for q in range(4):
        for f in range(4):
            off = (q // 2) * 64 + f * 16 + (q % 2) * 4
            hit = jnp.logical_or(base == off, base == off + 8)
            sel[q, :, f * PIECE : (f + 1) * PIECE] = jnp.where(hit, 1.0, 0.0).astype(BF16)

    xfs = (xf0, xf1)
    load_x.wait()
    load_tapf.wait()
    load_tapr.wait()

    @pl.when(has_right)
    def _():
        to_right.wait_send()
        to_left.wait_recv()

    @pl.when(has_left)
    def _():
        to_right.wait_recv()
        to_left.wait_send()

    def conv(cols, xf):
        xf[...] = xpad[:, cols].astype(F32)
        fw = tapf[:, cols]
        rv = tapr[:, cols]
        for r in range(0, BLOCK, STRIP):
            ahead = behind = None
            for k in range(WIDTH):
                a = fw[k : k + 1] * xf[pl.ds(HALO + r + k - (WIDTH - 1), STRIP), :]
                b = rv[k : k + 1] * xf[pl.ds(HALO + r + WIDTH - 1 - k, STRIP), :]
                ahead = a if ahead is None else ahead + a
                behind = b if behind is None else behind + b
            yield r, silu(ahead).astype(BF16), silu(behind).astype(BF16)

    for which in range(2):
        for r, a, b in conv(pl.ds(INNER + which * STATE, STATE), xfs[which]):
            kq[which, r : r + STRIP, :] = a
            kq[2 + which, r : r + STRIP, :] = b
    for i in range(2):
        keys = jnp.transpose(kq[2 * i].astype(F32)).astype(BF16)
        kt[i] = keys
        inside = row_i >= col_i if i == 0 else row_i <= col_i
        (gf_ref, gr_ref)[i][...] = jnp.where(inside, dot(kq[2 * i + 1], keys), 0.0).astype(BF16)
    load_gate.wait()

    lane = lax.broadcasted_iota(jnp.int32, (1, STATE), 1)
    first_half = lane < HEAD_DIM

    def convolve(p):
        for c in range(PIECE // STATE):
            cols = pl.ds(pl.multiple_of(p * PIECE + c * STATE, STATE), STATE)
            for r, a, b in conv(cols, xfs[c]):
                at = r // half * BLOCK + r % half
                vcat[p, pl.ds(at, STRIP), pl.ds(c * STATE, STATE)] = a
                vcat[p, pl.ds(half + at, STRIP), pl.ds(c * STATE, STATE)] = b

    def states(p):
        v = p // 4
        q = lax.rem(p, 4)
        for i in range(2):
            ends = dot(aft[v, i * half + half - 16 : (i + 1) * half, :], sel[q, :, 2 * PIECE : 3 * PIECE])
            drow[p, i : i + 1, :] = ends[15:16, :]
        for i, mid in enumerate((midf, midr)):
            parts = []
            for at, rows in ((i * half, lo), (BLOCK + i * half, hi)):
                wide = dot(aft[v, rows, :], sel[q, :, i * PIECE : (i + 1) * PIECE])
                weighted = (vcat[p, at : at + half, :].astype(F32) * wide).astype(BF16)
                parts.append(dot(kt[i, :, rows], weighted))
            first, second = parts if i == 0 else parts[::-1]
            mid[p] = first
            st[i, p] = second + drow[p, 1 - i : 2 - i, :] * first

        whole = drow[p, 0:1, :] * drow[p, 1:2, :]
        high = whole.astype(BF16).astype(F32)
        row = lax.broadcasted_iota(jnp.int32, (16, PIECE), 0)
        tail = jnp.where(row == 0, high, jnp.where(row == 1, whole - high, 0.0))
        give[p, 0:STATE, :] = st[other, p].astype(BF16)
        give[p, STATE:, :] = tail.astype(BF16)
        to_partner(p).start()

    def to_partner(p):
        return pltpu.make_async_remote_copy(
            src_ref=give.at[p],
            dst_ref=peer_in.at[p],
            send_sem=peer_send.at[p],
            recv_sem=peer_recv.at[p],
            device_id={"seq": partner},
            device_id_type=MESH,
        )

    def to_chip(p):
        return pltpu.make_async_remote_copy(
            src_ref=out_sb.at[p],
            dst_ref=chain_in.at[p],
            send_sem=chain_send.at[p],
            recv_sem=chain_recv.at[p],
            device_id={"seq": onward},
            device_id_type=MESH,
        )

    def to_entry(p):
        return pltpu.make_async_remote_copy(
            src_ref=chain_in.at[p],
            dst_ref=ent.at[mine, p],
            send_sem=ent_send.at[p],
            recv_sem=ent_recv.at[p],
            device_id={"seq": partner},
            device_id_type=MESH,
        )

    def relay(p):
        to_partner(p).wait_recv()

        @pl.when(takes)
        def _():
            to_chip(p).wait_recv()
            to_entry(p).start()

        beside = peer_in[p, STATE : STATE + 16, :].astype(F32)
        beside = beside[0:1] + beside[1:2]
        entry = peer_in[p, 0:STATE, :].astype(F32) + beside * chain_in[p].astype(F32)
        whole = drow[p, 0:1, :] * drow[p, 1:2, :]

        @pl.when(gives)
        def _():
            out_sb[p] = (st[mine, p] + whole * entry).astype(BF16)
            to_chip(p).start()

        ent[mine, p] = entry.astype(BF16)

    def within(p):
        for pair in range(PER // 2):
            lanes = slice(pair * STATE, (pair + 1) * STATE)
            tops, lows = [], []
            for j in (2 * pair, 2 * pair + 1):
                cft = jnp.broadcast_to(colc[p, :, j : j + 1], (BLOCK, half))
                cet = jnp.broadcast_to(colc[p, :, 64 + j : 65 + j], (BLOCK, half))
                ra = rowc[p, j : j + 1, :]
                rb = rowc[p, PER + j : PER + j + 1, :]
                for part, rows in ((tops, lo), (lows, hi)):
                    d = jnp.minimum(cft[rows] - ra[:, rows], rb[:, rows] - cet[rows])
                    d = jnp.exp(d).astype(BF16)
                    part.append(jnp.concatenate([gf_ref[rows, rows] * d, gr_ref[rows, rows] * d], axis=1))
            skip_row = jnp.where(first_half, skip[p * PER + 2 * pair], skip[p * PER + 2 * pair + 1])
            for part, rows, at in ((tops, lo, 0), (lows, hi, BLOCK)):
                res = dot(jnp.concatenate(part, axis=0), vcat[p, at : at + BLOCK, lanes])
                direct = skip_row * vcat[p, at : at + half, lanes].astype(F32)
                accw[p, rows, lanes] = direct + jnp.where(first_half, res[:half], res[half:])

    def y_copy(p):
        cols = pl.ds(pl.multiple_of(p * PIECE, PIECE), PIECE)
        return pltpu.make_async_copy(y_v.at[p], y_hbm.at[:, cols], out_sem.at[p])

    def finish(p):
        v = p // 4
        q = lax.rem(p, 4)
        cols = pl.ds(pl.multiple_of(p * PIECE, PIECE), PIECE)
        ef = ent[0, p]
        er = ent[1, p]
        late_f = (midf[p] + drow[p, 0:1, :] * ef.astype(F32)).astype(BF16)
        late_r = (midr[p] + drow[p, 1:2, :] * er.astype(F32)).astype(BF16)
        for rows, f, r in ((lo, ef, late_r), (hi, late_f, er)):
            y = accw[p, rows, :]
            grow = dot(aft[v, rows, :], sel[q, :, 2 * PIECE : 3 * PIECE])
            y = y + grow * dot(kq[1, rows, :], f)
            grow = dot(aft[v, rows, :], sel[q, :, 3 * PIECE : 4 * PIECE])
            y = y + grow * dot(kq[3, rows, :], r)
            y = y * silu(gate_v[rows, cols].astype(F32))
            y_v[p, rows, :] = y.astype(BF16)
            y = y * y
            ssq[rows, :] = ssq[rows, :] + (y[:, :STATE] + y[:, STATE:])
        y_copy(p).start()

    ssq[...] = jnp.zeros_like(ssq)
    late = 1 + PAIR + LAG * far_mine
    ready = jnp.maximum(jnp.maximum(PIECES + 1, late), 1 + 2 * PAIR + LAG * far_other)

    def relays(k):
        @pl.when(jnp.logical_and(k >= late, k < late + PIECES))
        def _():
            relay(k - late)

        @pl.when(jnp.logical_and(jnp.logical_and(k >= ready, k < ready + PIECES), fed))
        def _():
            to_entry(k - ready).wait_recv()

    convolve(0)

    def slot_a(k, carry):
        states(k - 1)
        convolve(k)
        relays(k)
        return carry

    lax.fori_loop(1, PIECES, slot_a, 0)
    states(PIECES - 1)

    def slot_b(k, carry):
        relays(k)

        @pl.when(k >= ready)
        def _():
            finish(k - ready)
            within(k - PIECES)

        @pl.when(k < ready)
        def _():
            within(k - PIECES)

        return carry

    lax.fori_loop(PIECES, 2 * PIECES, slot_b, 0)

    def slot_c(k, carry):
        relays(k)

        @pl.when(k >= ready)
        def _():
            finish(k - ready)

        return carry

    lax.fori_loop(2 * PIECES, ready + PIECES, slot_c, 0)
    mean = jnp.sum(ssq[...], axis=1, keepdims=True) * (1.0 / INNER)
    scale_ref[...] = jnp.broadcast_to(lax.rsqrt(mean + 1e-05), scale_ref.shape)

    def done(p, carry):
        to_partner(p).wait_send()

        @pl.when(gives)
        def _():
            to_chip(p).wait_send()

        @pl.when(takes)
        def _():
            to_entry(p).wait_send()

        return carry

    lax.fori_loop(0, PIECES, done, 0)

    def stored(p, carry):
        y_copy(p).wait()
        return carry

    lax.fori_loop(0, PIECES, stored, 0)


def scale_rows(y_hbm, scale_ref, gain_ref, out_hbm, y_v, out_v, in_sem, out_sem):
    parts = [pl.ds(r, TAIL) for r in range(0, BLOCK, TAIL)]
    loads = [pltpu.make_async_copy(y_hbm.at[s], y_v.at[s], in_sem.at[i]) for i, s in enumerate(parts)]
    stores = [
        pltpu.make_async_copy(out_v.at[s], out_hbm.at[s], out_sem.at[i]) for i, s in enumerate(parts)
    ]
    for load in loads:
        load.start()
    for i, rows in enumerate(parts):
        loads[i].wait()
        scale = scale_ref[rows, :]
        for c in range(0, INNER, STATE):
            cols = pl.ds(c, STATE)
            out_v[rows, cols] = (y_v[rows, cols].astype(F32) * scale * gain_ref[:, cols]).astype(BF16)
        stores[i].start()
    for store in stores:
        store.wait()


def per_device(
    mixer_input, gate_input, conv_forward, conv_reverse, step_size, decay_rate, skip_scale, norm_gain
):
    n = lax.axis_size("seq")
    vmem = pl.BlockSpec(memory_space=pltpu.VMEM)
    smem = pl.BlockSpec(memory_space=pltpu.SMEM)
    hbm = pl.BlockSpec(memory_space=pl.ANY)
    piece = (PIECES, BLOCK, PIECE)
    state = (PIECES, STATE, PIECE)
    dma = pltpu.SemaphoreType.DMA
    y, scale = pl.pallas_call(
        functools.partial(kernel, n),
        out_shape=(
            jax.ShapeDtypeStruct((BLOCK, INNER), BF16),
            jax.ShapeDtypeStruct((BLOCK, STATE), F32),
        ),
        in_specs=[hbm, hbm, hbm, hbm, hbm, smem, smem],
        out_specs=(hbm, vmem),
        scratch_shapes=[
            pltpu.VMEM((WIDTH, INNER + 2 * STATE), F32),
            pltpu.VMEM((WIDTH, INNER + 2 * STATE), F32),
            pltpu.VMEM((HEADS, BLOCK), F32),
            pltpu.VMEM((BLOCK + 2 * HALO, INNER + 2 * STATE), BF16),
            pltpu.VMEM((BLOCK, INNER), BF16),
            pltpu.VMEM((PIECES, 2 * BLOCK, PIECE), BF16),
            pltpu.VMEM(piece, F32),
            pltpu.VMEM((2,) + state, F32),
            pltpu.VMEM(state, F32),
            pltpu.VMEM(state, F32),
            pltpu.VMEM(state, BF16),
            pltpu.VMEM((PIECES, STATE + 16, PIECE), BF16),
            pltpu.VMEM((2,) + state, BF16),
            pltpu.VMEM((PIECES, STATE + 16, PIECE), BF16),
            pltpu.VMEM(state, BF16),
            pltpu.VMEM((PIECES, BLOCK, STATE), F32),
            pltpu.VMEM((HEADS, BLOCK), F32),
            pltpu.VMEM((HEADS, BLOCK), F32),
            pltpu.VMEM((PIECES, 2 * PER, BLOCK), F32),
            pltpu.VMEM((PIECES // 4, BLOCK, STATE), BF16),
            pltpu.VMEM((4, STATE, 4 * PIECE), BF16),
            pltpu.VMEM((PIECES, 8, PIECE), F32),
            pltpu.VMEM((BLOCK, BLOCK), BF16),
            pltpu.VMEM((BLOCK, BLOCK), BF16),
            pltpu.VMEM((4, BLOCK, STATE), BF16),
            pltpu.VMEM((2, STATE, BLOCK), BF16),
            pltpu.VMEM((BLOCK, STATE), F32),
            pltpu.VMEM(piece, BF16),
            pltpu.VMEM((BLOCK + 2 * HALO, STATE), F32),
            pltpu.VMEM((BLOCK + 2 * HALO, STATE), F32),
            dma((5,)),
            dma((2,)),
            dma((2,)),
            dma((PIECES,)),
            dma((PIECES,)),
            dma((PIECES,)),
            dma((PIECES,)),
            dma((PIECES,)),
            dma((PIECES,)),
            dma((PIECES,)),
        ],
        compiler_params=pltpu.CompilerParams(
            collective_id=0, has_side_effects=True, vmem_limit_bytes=56 * 1024 * 1024
        ),
        cost_estimate=pl.CostEstimate(flops=3 * 10**9, bytes_accessed=7 * 10**6, transcendentals=10**7),
        name="mixer",
    )(
        mixer_input, gate_input, conv_forward, conv_reverse, step_size, decay_rate, skip_scale
    )
    dma = pltpu.SemaphoreType.DMA
    parts = BLOCK // TAIL
    return pl.pallas_call(
        scale_rows,
        out_shape=jax.ShapeDtypeStruct((BLOCK, INNER), BF16),
        in_specs=[hbm, vmem, vmem],
        out_specs=hbm,
        scratch_shapes=[
            pltpu.VMEM((BLOCK, INNER), BF16),
            pltpu.VMEM((BLOCK, INNER), BF16),
            dma((parts,)),
            dma((parts,)),
        ],
        compiler_params=pltpu.CompilerParams(vmem_limit_bytes=60 * 1024 * 1024),
        cost_estimate=pl.CostEstimate(flops=2 * 10**6, bytes_accessed=4 * 10**6, transcendentals=0),
        name="scale_rows",
    )(y, scale, norm_gain.reshape(1, INNER))


def solution(mesh):
    in_specs = (
        P(("row", "seq"), None),
        P(("row", "seq"), None),
        P(),
        P(),
        P(None, ("row", "seq")),
        P("row"),
        P(),
        P(),
    )
    out_specs = P(("row", "seq"), None)
    return jax.shard_map(
        per_device, mesh=mesh, in_specs=in_specs, out_specs=out_specs, check_vma=False
    )
```
